512 devices in a mesh: dp: 64 (over z, x, core), fsdp: 8 (over y).
Axes of the slice: x: 4, y: 8, z: 8, core: 2. Of those that a mesh axis runs over, the one named last changes fastest.
Arguments:
- waveform: float32 [4096, 400], P(('dp', 'fsdp')), may hold values from -6 to 6
- lengths: int32 [4096], P(('dp', 'fsdp')), may hold values from 200 to 400, as said below
- owner_of: int32 [4096], P(('dp', 'fsdp')), may hold values from 0 to 63, as said below
- targets: float32 [4096, 39], P(('dp', 'fsdp')), may hold values from -5 to 5
- first_weight: float32 [10, 512], replicated, may hold values from -2 to 2
- first_gain: float32 [512], replicated, may hold values from 0.1 to 1.9
- first_shift: float32 [512], replicated, may hold values from -3 to 3
- second_weight: bfloat16 [1536, 512], P('fsdp'), may hold values from -0.15625 to 0.15625
- second_gain: float32 [512], replicated, may hold values from 0.1 to 1.9
- second_shift: float32 [512], replicated, may hold values from -3 to 3
Outputs:
- logvar: float32 [4096, 39], P(('dp', 'fsdp'))
- loss: float32 [], replicated
- grad_second_weight: float32 [1536, 512], P('fsdp')
- grad_first_weight: float32 [10, 512], replicated
- grad_first_gain: float32 [512], replicated
- grad_first_shift: float32 [512], replicated
- grad_second_gain: float32 [512], replicated
- grad_second_shift: float32 [512], replicated
The draws below stay inside these ranges and needn't reach their ends.
Inputs may be any that keep to these rules, and one draw needn't show every extreme that they name: `lengths`: every draw has a row of length 400 and one of length 200. `owner_of`: rows read by the devices of one fsdp index go to owners of the same fsdp index. From one reader, each owner receives either no row or exactly 1 row; every owner receives exactly 8 rows.
All inputs are finite; a program needn't handle non-finite values.
Results may differ from the reference program's by a relative error of at most 0.0019.
Values may be sent and summed in bfloat16 or wider, within the bound.
A program may use at most 64 MiB of HBM per device.

```python
import jax
import jax.numpy as jnp
from jax import lax

C = 512
LMAX = 400
RPD = 8
CAP = 1
F1 = 39
ROWS = 4096
N_DP = 64
N_FSDP = 8


def draw_lengths(key, part):
    first_key, second_key, third_key = jax.random.split(key, 3)
    shortest = LMAX // 2
    lengths_drawn = jax.random.randint(first_key, (ROWS,), shortest, LMAX + 1)
    top_row = jax.random.randint(second_key, (), 0, ROWS)
    bottom_row = (top_row + 1 + jax.random.randint(third_key, (), 0, ROWS - 1)) % ROWS
    positions = jnp.arange(ROWS)
    lengths_drawn = jnp.where(positions == top_row, LMAX, lengths_drawn)
    lengths_drawn = jnp.where(positions == bottom_row, shortest, lengths_drawn)
    return lengths_drawn.astype(jnp.int32)


def shuffled_slots(sub_key):
    return jax.random.permutation(sub_key, RPD)


def one_column(column_key):
    base_key, shift_key, shuffle_key = jax.random.split(column_key, 3)
    groups = RPD // CAP
    readers = jax.random.permutation(base_key, N_DP)
    offsets = jax.random.permutation(shift_key, N_DP)[:groups]
    shuffles = jax.vmap(shuffled_slots)(jax.random.split(shuffle_key, N_DP))
    return (readers[:, None] + offsets[shuffles // CAP]) % N_DP


def draw_owner_of(key, part):
    column_keys = jax.random.split(jax.random.fold_in(key, 17), N_FSDP)
    owners = jax.vmap(one_column)(column_keys)
    return jnp.transpose(owners, (1, 0, 2)).reshape(ROWS).astype(jnp.int32)


def level_of(own_key, shape, shards, low, high):
    gain, own = 1.0, jax.random.fold_in(own_key, 6)
    for position, shards_of in shards:
        heights = jnp.exp(jax.random.uniform(jax.random.fold_in(own, position), (shards_of,), jnp.float32, low / len(shards), high / len(shards)))
        gain = gain * jnp.repeat(heights, shape[position] // shards_of).reshape([-1 if axis == position else 1 for axis in range(len(shape))])
    return gain


def centred(rng, shape, deviation, reach, cuts=(), kind=jnp.bfloat16):
    result = deviation * jax.random.normal(rng, shape, jnp.float32)
    if cuts:
        result = result * level_of(rng, shape, cuts, -0.22, 0.18)
    return jnp.clip(result, -reach, reach).astype(kind)


def setup_inputs(seed: int = 0) -> dict:
    seeds = jax.random.split(jax.random.key(seed), 11)
    waveform = centred(seeds[0], (ROWS, LMAX), 1.0, 6.0, ((0, 512),), jnp.float32)
    lengths = draw_lengths(jax.random.fold_in(seeds[10], 71), 0)
    owner_of = draw_owner_of(jax.random.fold_in(seeds[10], 71), 0)
    targets = centred(seeds[3], (ROWS, F1), 1.0, 5.0, ((0, 512),), jnp.float32)
    first_weight = centred(seeds[4], (10, C), 10 ** -0.5, 2.0, (), jnp.float32)
    first_gain = jnp.clip(1.0 + 0.18 * jax.random.normal(seeds[5], (C,), jnp.float32), 0.1, 1.9)
    first_shift = centred(seeds[6], (C,), 0.5, 3.0, (), jnp.float32)
    second_weight = centred(seeds[7], (3 * C, C), (3 * C) ** -0.5, 0.15625, ((0, 8),))
    second_gain = jnp.clip(1.0 + 0.18 * jax.random.normal(seeds[8], (C,), jnp.float32), 0.1, 1.9)
    second_shift = centred(seeds[9], (C,), 0.5, 3.0, (), jnp.float32)
    return dict(waveform=waveform, lengths=lengths, owner_of=owner_of, targets=targets, first_weight=first_weight, first_gain=first_gain, first_shift=first_shift, second_weight=second_weight, second_gain=second_gain, second_shift=second_shift)


epsilon = 1e-05

def layer_norm(values, norm_gain, norm_shift):
    row_mean = lax.optimization_barrier(jnp.mean(values, axis=-1, keepdims=True))
    centered = values - row_mean
    row_var = lax.optimization_barrier(jnp.mean(centered * centered, axis=-1, keepdims=True))
    return centered * lax.rsqrt(row_var + epsilon) * norm_gain + norm_shift

def first_layer(waveform, first_weight, first_gain, first_shift):
    row_total, samples = waveform.shape
    frames = samples // 5 - 1
    blocks = waveform.reshape(row_total, samples // 5, 5)
    windows = jnp.concatenate([blocks[:, :frames], blocks[:, 1:frames + 1]], axis=2)
    pre_norm = jnp.dot(windows.reshape(row_total * frames, 10), first_weight, precision=lax.Precision.HIGHEST, preferred_element_type=jnp.float32)
    return jax.nn.gelu(layer_norm(pre_norm, first_gain, first_shift), approximate=False)

def make_patches(activated, row_total):
    channels = activated.shape[1]
    frames = activated.shape[0] // row_total
    later = (frames - 1) // 2
    shaped = activated.reshape(row_total, frames, channels)
    padded = jnp.concatenate([shaped, jnp.zeros((row_total, 1, channels), activated.dtype)], axis=1)
    paired = padded.reshape(row_total, later + 1, 2, channels)
    even_frames = paired[:, :, 0]
    odd_frames = paired[:, :, 1]
    joined = jnp.concatenate([even_frames[:, :later], odd_frames[:, :later], even_frames[:, 1:]], axis=2)
    return joined.reshape(row_total * later, 3 * channels)

def patch_grad(grad_patches, row_total, frames):
    channels = grad_patches.shape[1] // 3
    later = grad_patches.shape[0] // row_total
    shaped = grad_patches.reshape(row_total, later, 3, channels)
    zero_frame = jnp.zeros((row_total, 1, channels), grad_patches.dtype)
    even_frames = jnp.concatenate([shaped[:, :, 0], zero_frame], axis=1) + jnp.concatenate([zero_frame, shaped[:, :, 2]], axis=1)
    odd_frames = jnp.concatenate([shaped[:, :, 1], zero_frame], axis=1)
    paired = jnp.stack([even_frames, odd_frames], axis=2).reshape(row_total, 2 * later + 2, channels)
    return paired[:, :frames].reshape(row_total * frames, channels)

def frame_mask_of(row_lengths, later):
    first_valid = (row_lengths - 10) // 5 + 1
    second_valid = (first_valid - 3) // 2 + 1
    inside = jnp.arange(later, dtype=jnp.int32)[None, :] < second_valid[:, None]
    return inside.astype(jnp.float32).reshape(-1)

def head_loss(second_pre, second_gain, second_shift, target_flat, frame_mask):
    activated = jax.nn.gelu(layer_norm(second_pre, second_gain, second_shift), approximate=False)
    row_mean = lax.optimization_barrier(jnp.mean(activated, axis=-1, keepdims=True))
    centered = activated - row_mean
    raw_logvar = jnp.log(lax.optimization_barrier(jnp.mean(centered * centered, axis=-1)) + epsilon)
    misfit = raw_logvar - target_flat
    return (jnp.sum(frame_mask * misfit * misfit), raw_logvar)

def reference(waveform, lengths, owner_of, targets, first_weight, first_gain, first_shift, second_weight, second_gain, second_shift):
    row_total = waveform.shape[0]
    positions = jnp.arange(row_total, dtype=jnp.int32)
    column = positions // RPD % N_FSDP
    sort_keys = (owner_of * N_FSDP + column) * row_total + positions
    row_order = jnp.argsort(sort_keys).astype(jnp.int32)
    owned_wave = jnp.take(waveform, row_order, axis=0)
    owned_length = jnp.take(lengths, row_order, axis=0)
    block_count = row_total // RPD
    later = LMAX // 10 - 1
    frames = LMAX // 5 - 1
    channels = first_weight.shape[1]
    wave_blocks = owned_wave.reshape(block_count, RPD, LMAX)
    length_blocks = owned_length.reshape(block_count, RPD)
    target_blocks = targets.reshape(block_count, RPD, later)

    def one_block(carried, block_item):
        wave_block, length_block, target_block = block_item

        def first_part(weight_first, gain_first, shift_first):
            return first_layer(wave_block, weight_first, gain_first, shift_first)
        activated, first_pull = jax.vjp(first_part, first_weight, first_gain, first_shift)
        rounded = activated.astype(jnp.bfloat16)
        patches = make_patches(rounded, RPD)
        second_pre = jnp.dot(patches, second_weight, preferred_element_type=jnp.float32)
        frame_mask = frame_mask_of(length_block, later)

        def head_part(pre_norm, gain_second, shift_second):
            return head_loss(pre_norm, gain_second, shift_second, target_block.reshape(-1), frame_mask)
        loss_sum, head_pull, raw_logvar = jax.vjp(head_part, second_pre, second_gain, second_shift, has_aux=True)
        grad_pre, grad_gain_two, grad_shift_two = head_pull(jnp.ones_like(loss_sum))
        grad_pre = grad_pre.astype(jnp.bfloat16)
        grad_weight_two = lax.dot_general(patches, grad_pre, (((0,), (0,)), ((), ())), preferred_element_type=jnp.float32)
        grad_patches = lax.dot_general(grad_pre, second_weight, (((1,), (1,)), ((), ())), preferred_element_type=jnp.float32)
        grad_act = patch_grad(grad_patches, RPD, frames)
        grad_weight_one, grad_gain_one, grad_shift_one = first_pull(grad_act)
        updated = (carried[0] + grad_weight_two, carried[1] + grad_weight_one, carried[2] + grad_gain_one, carried[3] + grad_shift_one, carried[4] + grad_gain_two, carried[5] + grad_shift_two, carried[6] + loss_sum, carried[7] + jnp.sum(frame_mask))
        return (updated, (raw_logvar * frame_mask).reshape(RPD, later))
    start_state = (jnp.zeros((3 * channels, channels), jnp.float32), jnp.zeros((10, channels), jnp.float32), jnp.zeros((channels,), jnp.float32), jnp.zeros((channels,), jnp.float32), jnp.zeros((channels,), jnp.float32), jnp.zeros((channels,), jnp.float32), jnp.zeros((), jnp.float32), jnp.zeros((), jnp.float32))
    final_state, logvar_blocks = lax.scan(one_block, start_state, (wave_blocks, length_blocks, target_blocks))
    logvar = logvar_blocks.reshape(row_total, later)
    loss = final_state[6] / final_state[7]
    return (logvar, loss, final_state[0], final_state[1], final_state[2], final_state[3], final_state[4], final_state[5])
```

```python
import functools

import jax
import jax.numpy as jnp
from jax import lax
from jax.experimental import pallas as pl
from jax.experimental.pallas import tpu as pltpu
from jax.sharding import Mesh
from jax.sharding import PartitionSpec as P

DP = ("dp_0", "dp_1", "dp_2")
DP_FSDP = ("dp_0", "dp_1", "dp_2", "fsdp")
AXES = {"z": "dp_0", "x": "dp_1", "c": "dp_2", "y": "fsdp"}
EPS = 1e-05
C = 512
F32 = jnp.float32
BF16 = jnp.bfloat16
MESH = pl.DeviceIdType.MESH
TN = (((0,), (0,)), ((), ()))
NT = (((1,), (1,)), ((), ()))
TILES = 16
CHUNK = 32


class Exchange:
    def __init__(self, axis, size, me, src, dst, sems):
        self.axis, self.size, self.me = axis, size, me
        self.src, self.dst = src, dst
        self.send_sems, self.recv_sems = sems

    def _copy(self, r, slot, peer):
        return pltpu.make_async_remote_copy(
            src_ref=self.src(peer),
            dst_ref=self.dst(slot),
            send_sem=self.send_sems.at[r],
            recv_sem=self.recv_sems.at[r],
            device_id={AXES[self.axis]: peer},
            device_id_type=MESH,
        )

    def start(self):
        for r in range(1, self.size):
            self._copy(r, self.me, lax.rem(self.me + r, self.size)).start()

    def sender(self, r):
        return lax.rem(self.me + self.size - r, self.size)

    def wait_recv(self, r):
        s = self.sender(r)
        self._copy(r, s, s).wait_recv()

    def wait_all_recv(self):
        for r in range(1, self.size):
            self.wait_recv(r)

    def wait_sends(self):
        for r in range(1, self.size):
            self._copy(r, self.me, lax.rem(self.me + r, self.size)).wait_send()


def dot(a, b, dims=(((1,), (0,)), ((), ()))):
    return lax.dot_general(a, b, dims, preferred_element_type=F32)


def split2(v):
    hi = v.astype(BF16)
    return hi, (v - hi.astype(F32)).astype(BF16)


def split3(v):
    hi, mid = split2(v)
    return hi, mid, (v - hi.astype(F32) - mid.astype(F32)).astype(BF16)


def gelu_parts(u):
    a = jnp.abs(u)
    t = 1.0 / (1.0 + 0.23164190 * a)
    e = jnp.exp(u * u * -0.5)
    poly = 0.5 * 1.061405429
    poly = poly * t - 0.5 * 1.453152027
    poly = poly * t + 0.5 * 1.421413741
    poly = poly * t - 0.5 * 0.284496736
    poly = poly * t + 0.5 * 0.254829592
    tail = poly * t * e
    cdf = jnp.where(u >= 0.0, 1.0 - tail, tail)
    return u * cdf, cdf + u * (e * 0.3989422804014327)


def fold8(v):
    return v.reshape(v.shape[0] // 8, 8, v.shape[1]).sum(axis=0)


def kernel(sizes, *refs):
    Z, X, Y = sizes
    (wave_ref, blk_ref, fw_ref, g1_ref, s1_ref, w_ref, g2_ref, s2_ref,
     lv_ref, loss_ref, gw2_ref, gw1_ref, gg1_ref, gs1_ref, gg2_ref, gs2_ref,
     W, TG, LG, wpad, wconv, xcol, xh, dg, rs, act, act_peer, v, tsel, vmask, gf, G, g_peer,
     DA, DB, RA, RB, A1, B1, RA2, RB2, XR, dact, gph, gpm, S, S_peer, SY, S1, SZ, SX, SA, pick,
     w_sy, w_ry, w_sx, w_rx, w_sc, w_rc, tx_s, tx_r, tz_s, tz_r, lx_s, lx_r, lz_s, lz_r,
     a_s, a_r, b_s, b_r, a2_s, a2_r, b2_s, b2_r, x_s, x_r, z_s, z_r,
     sy_s, sy_r, sz_s, sz_r, sx_s, sx_r, sa_s, sa_r, c_s, c_r) = refs
    z, x, c, y = (lax.axis_index(AXES[k]) for k in "zxcy")
    other = 1 - c
    RY = W.shape[1]
    RX = RY // X
    RZ = RY // Z
    rows = 8 * 40
    per_y = TILES // Y
    dp = Z * X * 2
    readers = dp * 8
    me_dp = (z * X + x) * 2 + c

    barrier = pltpu.get_barrier_semaphore()
    for axis, size, me in (("c", 2, c), ("x", X, x), ("y", Y, y), ("z", Z, z)):
        for r in range(1, size):
            pl.semaphore_signal(
                barrier, inc=1, device_id={AXES[axis]: lax.rem(me + r, size)}, device_id_type=MESH
            )

    def core_copy(k, src, dst):
        return pltpu.make_async_remote_copy(
            src_ref=src, dst_ref=dst, send_sem=c_s.at[k], recv_sem=c_r.at[k],
            device_id={AXES["c"]: other}, device_id_type=MESH,
        )

    half = pl.ds(pl.multiple_of(c * 256, 256), 256)
    other_half = pl.ds(pl.multiple_of(other * 256, 256), 256)

    W[y] = w_ref[...]
    TG[z, x, c] = blk_ref[...]
    quarter = pl.ds(pl.multiple_of(x * RX, RX), RX)

    def quarter_of(k):
        return pl.ds(pl.multiple_of(k * RX, RX), RX)

    pl.semaphore_wait(barrier, 1 + (X - 1) + (Y - 1) + (Z - 1))

    wy = Exchange("y", Y, y, lambda p: W.at[y, quarter, half], lambda s: W.at[s, quarter, half], (w_sy, w_ry))
    wy.start()

    def wx(k, slot):
        return Exchange(
            "x", X, x, lambda p: W.at[slot, quarter, half],
            lambda s: W.at[slot, quarter_of(s), half], (w_sx.at[k], w_rx.at[k]),
        )

    def wc_send(k, slot):
        return pltpu.make_async_remote_copy(
            src_ref=W.at[slot, :, half], dst_ref=W.at[slot, :, half], send_sem=w_sc.at[k],
            recv_sem=w_rc.at[k], device_id={AXES["c"]: other}, device_id_type=MESH,
        )

    def wc_recv(k, slot):
        return pltpu.make_async_remote_copy(
            src_ref=W.at[slot, :, other_half], dst_ref=W.at[slot, :, other_half], send_sem=w_sc.at[k],
            recv_sem=w_rc.at[k], device_id={AXES["c"]: other}, device_id_type=MESH,
        )

    tc_send = core_copy(0, TG.at[z, x, c], TG.at[z, x, c])
    tc_recv = core_copy(0, TG.at[z, x, other], TG.at[z, x, other])
    tc_send.start()
    tx = Exchange("x", X, x, lambda p: TG.at[z, x], lambda s: TG.at[z, s], (tx_s, tx_r))
    tz = Exchange("z", Z, z, lambda p: TG.at[z], lambda s: TG.at[s], (tz_s, tz_r))

    wpad[...] = jnp.zeros_like(wpad)
    wpad[:, : wave_ref.shape[1]] = wave_ref[...]
    samples = lax.broadcasted_iota(jnp.int32, (512, 128), 0).astype(F32)
    lanes = lax.broadcasted_iota(jnp.int32, (512, 128), 1).astype(F32)
    tap = samples - 5.0 * jnp.floor((samples + 0.5) * 0.2)
    place_hi = jnp.where((lanes == tap) | (lanes == tap + 16.0), 1.0, 0.0).astype(BF16)
    place_mid = jnp.where(lanes == tap + 8.0, 1.0, 0.0).astype(BF16)
    frame = lax.broadcasted_iota(jnp.int32, (40, 512), 0)
    offset = lax.broadcasted_iota(jnp.int32, (40, 512), 1) - 10 * frame
    in_even = (offset >= 0) & (offset < 5)
    in_odd = (offset >= 5) & (offset < 10)
    even, odd = [], []
    for k in range(8):
        row = jnp.broadcast_to(wpad[k : k + 1, :], (40, 512))
        even.append(jnp.where(in_even, row, 0.0))
        odd.append(jnp.where(in_odd, row, 0.0))
    blocks = []
    for parts in (even, odd):
        hi, mid = split2(jnp.concatenate(parts, axis=0))
        blocks.append(dot(hi, place_hi) + dot(mid, place_mid))
    even_block, odd_block = blocks
    xcol[:rows] = (even_block + pltpu.roll(odd_block, 32, 1)).astype(BF16)
    xcol[rows:] = (odd_block + pltpu.roll(pltpu.roll(even_block, rows - 1, 0), 32, 1)).astype(BF16)
    wconv[...] = jnp.zeros_like(wconv)
    fw = fw_ref[...]
    fw_hi = fw.astype(BF16).astype(F32)
    fw_mid = (fw - fw_hi).astype(BF16).astype(F32)
    for base, taps in ((0, slice(0, 5)), (32, slice(5, 10))):
        wconv[base : base + 5] = fw_hi[taps]
        wconv[base + 8 : base + 13] = fw_hi[taps]
        wconv[base + 16 : base + 21] = fw_mid[taps]
    xh[...] = dot(xcol[...], wconv[...].astype(BF16))

    g1, s1 = g1_ref[...], s1_ref[...]

    def forward_chunk(i, carry):
        at = pl.ds(pl.multiple_of(i * CHUNK, CHUNK), CHUNK)
        pre = xh[at, :]
        centered = pre - jnp.mean(pre, axis=1, keepdims=True)
        inv = lax.rsqrt(jnp.mean(centered * centered, axis=1, keepdims=True) + EPS)
        normed = centered * inv
        value, slope = gelu_parts(normed * g1 + s1)
        xh[at, :] = normed
        dg[at, :] = slope
        rs[at, :] = jnp.broadcast_to(inv, (CHUNK, 128))
        act[at, :] = value.astype(BF16)
        return carry

    chunks = 2 * rows // CHUNK
    lax.fori_loop(0, chunks // 2, forward_chunk, 0)
    tc_recv.wait_recv()
    tx.start()
    for r in range(1, Y):
        wy.wait_recv(r)
        wx(r, wy.sender(r)).start()
    lax.fori_loop(chunks // 2, chunks, forward_chunk, 0)
    act_send = core_copy(1, act, act_peer)
    act_send.start()
    tx.wait_all_recv()
    tz.start()
    for r in range(1, Y):
        slot = wy.sender(r)
        wx(r, slot).wait_all_recv()
        wc_send(r, slot).start()

    tz.wait_all_recv()
    table = TG[...].reshape(readers, 128)
    owner_col = table[:, 39:40]
    r8 = lax.broadcasted_iota(jnp.int32, (8, 128), 0)
    l8 = lax.broadcasted_iota(jnp.int32, (8, 128), 1)
    mine = blk_ref[...]
    owner_row = jnp.sum(jnp.where(r8 == l8, mine[:, 39:40], 0.0), axis=0, keepdims=True)
    rr = lax.broadcasted_iota(jnp.int32, (readers, 128), 0)
    ll = lax.broadcasted_iota(jnp.int32, (readers, 128), 1)
    before = jnp.sum(
        jnp.where((owner_col == owner_row) & (rr < me_dp * 8), 1.0, 0.0), axis=0, keepdims=True
    )
    wanted = owner_row * 8.0 + before
    one_hot = jnp.where((rr.astype(F32) == wanted) & (ll < 8), 1.0, 0.0).astype(BF16)
    found = sum(dot(one_hot, part, TN) for part in split3(table))
    tsel[...] = found[:8]
    vmask[...] = jnp.where(l8.astype(F32) < mine[:, 40:41], 1.0, 0.0)
    flags = jnp.where(owner_col == me_dp.astype(F32), 1.0, 0.0)
    flags = jnp.broadcast_to(flags, (readers, 128))
    lower = lax.broadcasted_iota(jnp.int32, (readers, readers), 0) > lax.broadcasted_iota(
        jnp.int32, (readers, readers), 1
    )
    place = dot(jnp.where(lower, 1.0, 0.0).astype(BF16), flags.astype(BF16))
    pick[...] = jnp.where((flags > 0.5) & (place == ll.astype(F32)), 1.0, 0.0).astype(BF16)

    for r in range(1, Y):
        slot = wy.sender(r)
        wc_recv(r, slot).wait_recv()

    def tap_weight(q):
        return W[...].reshape(3 * C, C)[q * C : (q + 1) * C]

    act_even, act_odd = act[:rows], act[rows:]
    later = dot(act_even, tap_weight(2))
    v[...] = dot(act_even, tap_weight(0)) + dot(act_odd, tap_weight(1)) + pltpu.roll(later, rows - 1, 0)

    g2, s2 = g2_ref[...], s2_ref[...]
    eye = lax.broadcasted_iota(jnp.int32, (40, 128), 0) == lax.broadcasted_iota(jnp.int32, (40, 128), 1)

    def head_row(k, carry):
        gain_sum, shift_sum, misfit_sum, count = carry
        at = pl.ds(pl.multiple_of(k * 40, 8), 40)
        target = jnp.sum(jnp.where(eye, tsel[pl.ds(k, 1), :], 0.0), axis=1, keepdims=True)
        mask = jnp.sum(jnp.where(eye, vmask[pl.ds(k, 1), :], 0.0), axis=1, keepdims=True)
        pre = v[at, :]
        centered = pre - jnp.mean(pre, axis=1, keepdims=True)
        inv = lax.rsqrt(jnp.mean(centered * centered, axis=1, keepdims=True) + EPS)
        normed = centered * inv
        value, slope = gelu_parts(normed * g2 + s2)
        centered = value - jnp.mean(value, axis=1, keepdims=True)
        spread = jnp.mean(centered * centered, axis=1, keepdims=True) + EPS
        raw = jnp.log(spread)
        misfit = raw - target
        LG[z, x, c, pl.ds(k, 1), :] = jnp.sum(jnp.where(eye, raw * mask, 0.0), axis=0, keepdims=True)
        du = centered * (mask * misfit * (4.0 / C) / spread) * slope
        dx = du * g2
        m1 = jnp.mean(dx, axis=1, keepdims=True)
        m2 = jnp.mean(dx * normed, axis=1, keepdims=True)
        gf[at, :] = inv * (dx - m1 - normed * m2)
        return (
            gain_sum + fold8(du * normed),
            shift_sum + fold8(du),
            misfit_sum + mask * misfit * misfit,
            count + mask,
        )

    zero = jnp.zeros((8, C), F32)
    column = jnp.zeros((40, 1), F32)
    gain_sum2, shift_sum2, misfit_sum, count = lax.fori_loop(0, 8, head_row, (zero, zero, column, column))
    lc_send = core_copy(3, LG.at[z, x, c], LG.at[z, x, c])
    lc_recv = core_copy(3, LG.at[z, x, other], LG.at[z, x, other])
    lc_send.start()
    grad = gf[...]
    grad_late = pltpu.roll(grad, 1, 0)
    for h in range(2):
        G[h, 0] = grad[:, 256 * h : 256 * (h + 1)].astype(BF16)
        G[h, 1] = grad_late[:, 256 * h : 256 * (h + 1)].astype(BF16)
    g_send = core_copy(2, G.at[other], g_peer)
    g_send.start()

    def column_grads(acts, grads):
        e, o = acts[:rows], acts[rows:]
        return dot(e, grads[0], TN), dot(o, grads[0], TN), dot(e, grads[1], TN)

    own = column_grads(act, G.at[c])
    lx = Exchange("x", X, x, lambda p: LG.at[z, x], lambda s: LG.at[z, s], (lx_s, lx_r))
    lz = Exchange("z", Z, z, lambda p: LG.at[z], lambda s: LG.at[s], (lz_s, lz_r))
    act_send.wait_recv()
    g_send.wait_recv()
    peers = column_grads(act_peer, g_peer)
    total = jnp.concatenate([a + b for a, b in zip(own, peers)], axis=0)
    DA[...] = total[:, :128].reshape(Y, RY, 128)
    DB[...] = total[:, 128:].reshape(Y, Z, RZ, 128)
    ya = Exchange("y", Y, y, lambda p: DA.at[p], lambda s: RA.at[s], (a_s, a_r))
    zb = Exchange("z", Z, z, lambda p: DB.at[:, p], lambda s: RB.at[s], (b_s, b_r))
    ya.start()
    zb.start()
    lc_recv.wait_recv()
    lx.start()

    def whole_grad(k):
        return jnp.concatenate([G[0, k], G[1, k]], axis=1)

    now, late = whole_grad(0), whole_grad(1)
    dact[:rows] = dot(now, tap_weight(0), NT) + dot(late, tap_weight(2), NT)
    dact[rows:] = dot(now, tap_weight(1), NT)

    def backward_chunk(i, carry):
        gain_sum, shift_sum = carry
        at = pl.ds(pl.multiple_of(i * CHUNK, CHUNK), CHUNK)
        normed = xh[at, :]
        du = dact[at, :] * dg[at, :]
        dx = du * g1
        m1 = jnp.mean(dx, axis=1, keepdims=True)
        m2 = jnp.mean(dx * normed, axis=1, keepdims=True)
        dpre = rs[at, :1] * (dx - m1 - normed * m2)
        hi, mid = split2(dpre)
        gph[at, :] = hi
        gpm[at, :] = mid
        return gain_sum + fold8(du * normed), shift_sum + fold8(du)

    gain_sum1, shift_sum1 = lax.fori_loop(0, chunks, backward_chunk, (zero, zero))
    taps = dot(xcol[...], gph[...], TN) + dot(xcol[...], gpm[...], TN)
    ri = lax.broadcasted_iota(jnp.int32, (8, C), 0)
    li = lax.broadcasted_iota(jnp.int32, (8, C), 1)

    def line(vector, k):
        return jnp.where(ri == k, jnp.sum(vector, axis=0, keepdims=True), 0.0)

    loss_line = jnp.where(
        li == 0,
        jnp.sum(misfit_sum, axis=0, keepdims=True),
        jnp.where(li == 1, jnp.sum(count, axis=0, keepdims=True), 0.0),
    )
    groups = [
        taps[0:8] + taps[8:16],
        taps[32:40] + taps[40:48],
        line(gain_sum1, 0) + line(shift_sum1, 1) + line(gain_sum2, 2) + line(shift_sum2, 3)
        + jnp.where(ri == 4, loss_line, 0.0),
        zero,
    ]
    for i, group in enumerate(groups):
        for j in range(4):
            S[4 * i + j] = group[:, 128 * j : 128 * (j + 1)]
    sc = core_copy(4, S, S_peer)
    sc.start()
    lx.wait_all_recv()
    lz.start()
    sc.wait_recv()
    S1[...] = (S[...] + S_peer[...]).reshape(Y, per_y, 8, 128)
    sy = Exchange("y", Y, y, lambda p: S1.at[p], lambda s: SY.at[s], (sy_s, sy_r))
    sy.start()

    total = DA[y]
    for r in range(1, Y):
        ya.wait_recv(r)
        total = total + RA[ya.sender(r)]
    A1[...] = total.reshape(Z, RZ, 128)
    za = Exchange("z", Z, z, lambda p: A1.at[p], lambda s: RA2.at[s], (a2_s, a2_r))
    za.start()
    total = DB[:, z]
    for r in range(1, Z):
        zb.wait_recv(r)
        total = total + RB[zb.sender(r)]
    B1[...] = total
    yb = Exchange("y", Y, y, lambda p: B1.at[p], lambda s: RB2.at[s], (b2_s, b2_r))
    yb.start()
    sy.wait_all_recv()
    SY[y] = S1[y]
    total = SY[0]
    for k in range(1, Y):
        total = total + SY[k]
    SZ[z] = total
    sz = Exchange("z", Z, z, lambda p: SZ.at[z], lambda s: SZ.at[s], (sz_s, sz_r))
    sz.start()

    first = A1[z]
    for r in range(1, Z):
        za.wait_recv(r)
        first = first + RA2[za.sender(r)]
    second = B1[y]
    for r in range(1, Y):
        yb.wait_recv(r)
        second = second + RB2[yb.sender(r)]
    XR[x] = jnp.concatenate([first, second], axis=1)
    xs = Exchange("x", X, x, lambda p: XR.at[x], lambda s: XR.at[s], (x_s, x_r))
    xs.start()
    sz.wait_all_recv()
    total = SZ[0]
    for k in range(1, Z):
        total = total + SZ[k]
    SX[x] = total
    sx = Exchange("x", X, x, lambda p: SX.at[x], lambda s: SX.at[s], (sx_s, sx_r))
    sx.start()

    def rows_of(k):
        return pl.ds(pl.multiple_of(k * RZ, 8), RZ)

    xs.wait_all_recv()
    total = XR[0]
    for k in range(1, X):
        total = total + XR[k]
    gw2_ref[rows_of(z), half] = total
    zg = Exchange(
        "z", Z, z, lambda p: gw2_ref.at[rows_of(z), half], lambda s: gw2_ref.at[rows_of(s), half], (z_s, z_r)
    )
    zg.start()
    sx.wait_all_recv()
    total = SX[0]
    for k in range(1, X):
        total = total + SX[k]
    SA[y] = total
    sa = Exchange("y", Y, y, lambda p: SA.at[y], lambda s: SA.at[s], (sa_s, sa_r))
    sa.start()

    lz.wait_all_recv()
    logs = LG[...].reshape(readers, 128)
    picked = sum(dot(pick[...], part, TN) for part in split3(logs))
    lv_ref[...] = picked[:8, : lv_ref.shape[1]]

    zg.wait_all_recv()
    fin_send = core_copy(5, gw2_ref.at[:, half], gw2_ref.at[:, half])
    fin_recv = core_copy(5, gw2_ref.at[:, other_half], gw2_ref.at[:, other_half])
    fin_send.start()

    sa.wait_all_recv()
    done = SA[...].reshape(TILES, 8, 128)

    def wide(i):
        return jnp.concatenate([done[4 * i + j] for j in range(4)], axis=1)

    gw1_ref[0:5] = wide(0)[0:5]
    gw1_ref[5:10] = wide(1)[0:5]
    norms = wide(2)
    gg1_ref[...] = norms[0:1]
    gs1_ref[...] = norms[1:2]
    gg2_ref[...] = norms[2:3]
    gs2_ref[...] = norms[3:4]
    loss_ref[...] = norms[4:5, 0:1] / norms[4:5, 1:2]
    fin_recv.wait_recv()

    for e in (wy, tx, tz, lx, lz, ya, zb, za, yb, xs, zg, sy, sz, sx, sa):
        e.wait_sends()
    for r in range(1, Y):
        slot = wy.sender(r)
        wx(r, slot).wait_sends()
        wc_send(r, slot).wait_send()
    for copy in (tc_send, act_send, g_send, lc_send, sc, fin_send):
        copy.wait_send()


def per_device(sizes, waveform, lengths, owner_of, targets, first_weight, first_gain, first_shift,
               second_weight, second_gain, second_shift):
    Z, X, Y = sizes
    row_total, later = targets.shape
    valid = ((lengths - 10) // 5 - 2) // 2 + 1
    block = jnp.concatenate(
        [
            targets,
            owner_of.astype(F32)[:, None],
            valid.astype(F32)[:, None],
            jnp.zeros((row_total, 128 - later - 2), F32),
        ],
        axis=1,
    )
    RY = second_weight.shape[0]
    RZ = RY // Z
    rows = 320
    dma = pltpu.SemaphoreType.DMA
    vm = pltpu.VMEM
    per_y = TILES // Y
    scratch = [
        vm((Y, RY, C), BF16), vm((Z, X, 2, 8, 128), F32), vm((Z, X, 2, 8, 128), F32),
        vm((8, 512), F32), vm((128, C), F32), vm((2 * rows, 128), BF16),
        vm((2 * rows, C), F32), vm((2 * rows, C), F32), vm((2 * rows, 128), F32),
        vm((2 * rows, C), BF16), vm((2 * rows, C), BF16), vm((rows, C), F32),
        vm((8, 128), F32), vm((8, 128), F32), vm((rows, C), F32),
        vm((2, 2, rows, 256), BF16), vm((2, rows, 256), BF16),
        vm((Y, RY, 128), F32), vm((Y, Z, RZ, 128), F32), vm((Y, RY, 128), F32), vm((Z, Y, RZ, 128), F32),
        vm((Z, RZ, 128), F32), vm((Y, RZ, 128), F32), vm((Z, RZ, 128), F32), vm((Y, RZ, 128), F32),
        vm((X, RZ, 256), F32), vm((2 * rows, C), F32), vm((2 * rows, C), BF16), vm((2 * rows, C), BF16),
        vm((TILES, 8, 128), F32), vm((TILES, 8, 128), F32), vm((Y, per_y, 8, 128), F32),
        vm((Y, per_y, 8, 128), F32), vm((Z, per_y, 8, 128), F32), vm((X, per_y, 8, 128), F32),
        vm((Y, per_y, 8, 128), F32), vm((Z * X * 2 * 8, 128), BF16),
        dma((Y,)), dma((Y,)), dma((Y, X)), dma((Y, X)), dma((Y,)), dma((Y,)),
        dma((X,)), dma((X,)), dma((Z,)), dma((Z,)), dma((X,)), dma((X,)), dma((Z,)), dma((Z,)),
        dma((Y,)), dma((Y,)), dma((Z,)), dma((Z,)), dma((Z,)), dma((Z,)), dma((Y,)), dma((Y,)),
        dma((X,)), dma((X,)), dma((Z,)), dma((Z,)),
        dma((Y,)), dma((Y,)), dma((Z,)), dma((Z,)), dma((X,)), dma((X,)), dma((Y,)), dma((Y,)),
        dma((8,)), dma((8,)),
    ]
    shapes = [
        (row_total, later), (1, 1), (RY, C), (10, C), (1, C), (1, C), (1, C), (1, C),
    ]
    whole = pl.BlockSpec(memory_space=pltpu.VMEM)
    out = pl.pallas_call(
        functools.partial(kernel, sizes),
        out_shape=[jax.ShapeDtypeStruct(s, F32) for s in shapes],
        in_specs=[whole] * 8,
        out_specs=[whole] * len(shapes),
        scratch_shapes=scratch,
        compiler_params=pltpu.CompilerParams(
            collective_id=0, has_side_effects=True, vmem_limit_bytes=56 * 2**20
        ),
    )(
        waveform, block, first_weight, first_gain[None], first_shift[None], second_weight,
        second_gain[None], second_shift[None],
    )
    lv, loss, gw2, gw1, gg1, gs1, gg2, gs2 = out
    return lv, loss[0, 0], gw2, gw1, gg1[0], gs1[0], gg2[0], gs2[0]


def solution(mesh):
    dp, fsdp = mesh.shape["dp"], mesh.shape["fsdp"]
    x = 4 if dp >= 64 else 2
    z = dp // (2 * x)
    torus = Mesh(mesh.devices.reshape(z, x, 2, fsdp), ("dp_0", "dp_1", "dp_2", "fsdp"))
    return jax.shard_map(
        functools.partial(per_device, (z, x, fsdp)),
        mesh=torus,
        in_specs=(
            P(DP_FSDP, None), P(DP_FSDP), P(DP_FSDP), P(DP_FSDP, None), P(), P(), P(),
            P("fsdp", None), P(), P(),
        ),
        out_specs=(P(DP_FSDP, None), P(), P("fsdp", None), P(), P(), P(), P(), P()),
        check_vma=False,
    )
```

```python
import functools

import jax
import jax.numpy as jnp
from jax import lax
from jax.experimental import pallas as pl
from jax.experimental.pallas import tpu as pltpu
from jax.sharding import Mesh
from jax.sharding import PartitionSpec as P

DP = ("dp_0", "dp_1", "dp_2")
DP_FSDP = ("dp_0", "dp_1", "dp_2", "fsdp")
AXES = {"z": "dp_0", "x": "dp_1", "c": "dp_2", "y": "fsdp"}
EPS = 1e-05
C = 512
F32 = jnp.float32
BF16 = jnp.bfloat16
MESH = pl.DeviceIdType.MESH
TN = (((0,), (0,)), ((), ()))
NT = (((1,), (1,)), ((), ()))
TILES = 16
CHUNK = 32
LN2 = 0.6931471805599453
LOG2E = 1.4426950408889634


class Exchange:
    def __init__(self, axis, size, me, src, dst, sems):
        self.axis, self.size, self.me = axis, size, me
        self.src, self.dst = src, dst
        self.send_sems, self.recv_sems = sems

    def _copy(self, r, slot, peer):
        return pltpu.make_async_remote_copy(
            src_ref=self.src(peer),
            dst_ref=self.dst(slot),
            send_sem=self.send_sems.at[r],
            recv_sem=self.recv_sems.at[r],
            device_id={AXES[self.axis]: peer},
            device_id_type=MESH,
        )

    def start(self):
        for r in range(1, self.size):
            self._copy(r, self.me, lax.rem(self.me + r, self.size)).start()

    def sender(self, r):
        return lax.rem(self.me + self.size - r, self.size)

    def wait_recv(self, r):
        s = self.sender(r)
        self._copy(r, s, s).wait_recv()

    def wait_all_recv(self):
        for r in range(1, self.size):
            self.wait_recv(r)

    def wait_sends(self):
        for r in range(1, self.size):
            self._copy(r, self.me, lax.rem(self.me + r, self.size)).wait_send()


def dot(a, b, dims=(((1,), (0,)), ((), ()))):
    return lax.dot_general(a, b, dims, preferred_element_type=F32)


def split2(v):
    hi = v.astype(BF16)
    return hi, (v - hi.astype(F32)).astype(BF16)


def split3(v):
    hi, mid = split2(v)
    return hi, mid, (v - hi.astype(F32) - mid.astype(F32)).astype(BF16)


def gelu_parts(u):
    a = jnp.abs(u)
    t = 1.0 / (1.0 + 0.23164190 * a)
    e = jnp.exp(u * u * -0.5)
    poly = 0.5 * 1.061405429
    poly = poly * t - 0.5 * 1.453152027
    poly = poly * t + 0.5 * 1.421413741
    poly = poly * t - 0.5 * 0.284496736
    poly = poly * t + 0.5 * 0.254829592
    tail = poly * t * e
    cdf = jnp.where(u >= 0.0, 1.0 - tail, tail)
    return u * cdf, cdf + u * (e * 0.3989422804014327)


def fold8(v):
    return v.reshape(v.shape[0] // 8, 8, v.shape[1]).sum(axis=0)


def kernel(sizes, *refs):
    Z, X, Y = sizes
    (wave_ref, tgt_ref, own_ref, len_ref, fw_ref, g1_ref, s1_ref, w_ref, g2_ref, s2_ref,
     lv_ref, gw2_ref, small_ref,
     W, TG, LG, blk, wpad, wconv, xcol, xh, dg, rs, act, act_peer, v, tsel, vmask, gf, G, g_peer,
     DA, DB, QA, QB, RA, RB, A1, B1, RA2, RB2, XR, dact, gph, gpm, S, S_peer, SY, S1, SZ, SX, SA, pick,
     w_sy, w_ry, w_sx, w_rx, w_sc, w_rc, tx_s, tx_r, tz_s, tz_r, lx_s, lx_r, lz_s, lz_r,
     a_s, a_r, b_s, b_r, a2_s, a2_r, b2_s, b2_r, x_s, x_r, z_s, z_r,
     sy_s, sy_r, sz_s, sz_r, sx_s, sx_r, sa_s, sa_r, c_s, c_r) = refs
    z, x, c, y = (lax.axis_index(AXES[k]) for k in "zxcy")
    other = 1 - c
    RY = W.shape[1]
    RX = RY // X
    RZ = RY // Z
    rows = 8 * 40
    per_y = TILES // 2 // Y
    dp = Z * X * 2
    readers = dp * 8
    me_dp = (z * X + x) * 2 + c

    barrier = pltpu.get_barrier_semaphore()
    for axis, size, me in (("c", 2, c), ("x", X, x), ("y", Y, y), ("z", Z, z)):
        for r in range(1, size):
            pl.semaphore_signal(
                barrier, inc=1, device_id={AXES[axis]: lax.rem(me + r, size)}, device_id_type=MESH
            )

    def core_copy(k, src, dst):
        return Exchange("c", 2, c, lambda p: src, dst, (c_s.at[k], c_r.at[k]))

    half = pl.ds(pl.multiple_of(c * 256, 256), 256)

    W[y] = w_ref[...]
    r8 = lax.broadcasted_iota(jnp.int32, (8, 128), 0)
    l8 = lax.broadcasted_iota(jnp.int32, (8, 128), 1)
    numbers = jnp.zeros((8, 128), jnp.int32)
    for k in range(8):
        valid = ((len_ref[k] - 10) // 5 - 2) // 2 + 1
        numbers = jnp.where(r8 == k, jnp.where(l8 == 39, own_ref[k], valid), numbers)
    blk[...] = numbers.astype(F32)
    blk[:, : tgt_ref.shape[1]] = tgt_ref[...]
    TG[z, x, c] = blk[...]
    quarter = pl.ds(pl.multiple_of(x * RX, RX), RX)

    def quarter_of(k):
        return pl.ds(pl.multiple_of(k * RX, RX), RX)

    pl.semaphore_wait(barrier, 1 + (X - 1) + (Y - 1) + (Z - 1))

    wy = Exchange("y", Y, y, lambda p: W.at[y, quarter, half], lambda s: W.at[s, quarter, half], (w_sy, w_ry))
    wy.start()

    def wx(k, slot):
        return Exchange(
            "x", X, x, lambda p: W.at[slot, quarter, half],
            lambda s: W.at[slot, quarter_of(s), half], (w_sx.at[k], w_rx.at[k]),
        )

    def half_of(k):
        return pl.ds(pl.multiple_of(k * 256, 256), 256)

    def wc(k, slot):
        return Exchange(
            "c", 2, c, lambda p: W.at[slot, :, half], lambda s: W.at[slot, :, half_of(s)],
            (w_sc.at[k], w_rc.at[k]),
        )

    wxs = [wx(r, wy.sender(r)) for r in range(1, Y)]
    wcs = [wc(r, wy.sender(r)) for r in range(1, Y)]
    tz = Exchange("z", Z, z, lambda p: TG.at[z, x, c], lambda s: TG.at[s, x, c], (tz_s, tz_r))
    tz.start()
    tx = Exchange("x", X, x, lambda p: TG.at[:, x, c], lambda s: TG.at[:, s, c], (tx_s, tx_r))
    tc = core_copy(0, TG.at[:, :, c], lambda s: TG.at[:, :, s])

    wpad[...] = jnp.zeros_like(wpad)
    wpad[:, : wave_ref.shape[1]] = wave_ref[...]
    samples = lax.broadcasted_iota(jnp.int32, (512, 128), 0).astype(F32)
    lanes = lax.broadcasted_iota(jnp.int32, (512, 128), 1).astype(F32)
    tap = samples - 5.0 * jnp.floor((samples + 0.5) * 0.2)
    place_hi = jnp.where((lanes == tap) | (lanes == tap + 16.0), 1.0, 0.0).astype(BF16)
    place_mid = jnp.where(lanes == tap + 8.0, 1.0, 0.0).astype(BF16)
    frame = lax.broadcasted_iota(jnp.int32, (40, 512), 0)
    offset = lax.broadcasted_iota(jnp.int32, (40, 512), 1) - 10 * frame
    in_even = (offset >= 0) & (offset < 5)
    in_odd = (offset >= 5) & (offset < 10)
    even, odd = [], []
    for k in range(8):
        row = jnp.broadcast_to(wpad[k : k + 1, :], (40, 512))
        even.append(jnp.where(in_even, row, 0.0))
        odd.append(jnp.where(in_odd, row, 0.0))
    blocks = []
    for parts in (even, odd):
        hi, mid = split2(jnp.concatenate(parts, axis=0))
        blocks.append(dot(hi, place_hi) + dot(mid, place_mid))
    even_block, odd_block = blocks
    xcol[:rows] = (even_block + pltpu.roll(odd_block, 32, 1)).astype(BF16)
    xcol[rows:] = (odd_block + pltpu.roll(pltpu.roll(even_block, rows - 1, 0), 32, 1)).astype(BF16)
    wconv[...] = jnp.zeros_like(wconv)
    fw = fw_ref[...]
    fw_hi = fw.astype(BF16).astype(F32)
    fw_mid = (fw - fw_hi).astype(BF16).astype(F32)
    for base, taps in ((0, slice(0, 5)), (32, slice(5, 10))):
        wconv[base : base + 5] = fw_hi[taps]
        wconv[base + 8 : base + 13] = fw_hi[taps]
        wconv[base + 16 : base + 21] = fw_mid[taps]
    xh[...] = dot(xcol[...], wconv[...].astype(BF16))

    g1, s1 = g1_ref[...], s1_ref[...]

    def forward_chunk(i, carry):
        at = pl.ds(pl.multiple_of(i * CHUNK, CHUNK), CHUNK)
        pre = xh[at, :]
        centered = pre - jnp.mean(pre, axis=1, keepdims=True)
        inv = lax.rsqrt(jnp.mean(centered * centered, axis=1, keepdims=True) + EPS)
        normed = centered * inv
        value, slope = gelu_parts(normed * g1 + s1)
        xh[at, :] = normed
        dg[at, :] = slope
        rs[at, :] = jnp.broadcast_to(inv, (CHUNK, 128))
        act[at, :] = value.astype(BF16)
        return carry

    chunks = 2 * rows // CHUNK
    lax.fori_loop(0, chunks // 2, forward_chunk, 0, unroll=2)
    tz.wait_all_recv()
    tx.start()
    for r in range(1, Y):
        wy.wait_recv(r)
        wxs[r - 1].start()
    lax.fori_loop(chunks // 2, chunks, forward_chunk, 0, unroll=2)
    act_send = core_copy(1, act, lambda s: act_peer)
    act_send.start()
    tx.wait_all_recv()
    tc.start()
    for r in range(1, Y):
        wxs[r - 1].wait_all_recv()
        wcs[r - 1].start()

    tc.wait_all_recv()
    table = TG[...].reshape(readers, 128)
    owner_col = table[:, 39:40]
    mine = blk[...]
    owner_row = jnp.sum(jnp.where(r8 == l8, mine[:, 39:40], 0.0), axis=0, keepdims=True)
    rr = lax.broadcasted_iota(jnp.int32, (readers, 128), 0)
    ll = lax.broadcasted_iota(jnp.int32, (readers, 128), 1)
    before = jnp.sum(
        jnp.where((owner_col == owner_row) & (rr < me_dp * 8), 1.0, 0.0), axis=0, keepdims=True
    )
    wanted = owner_row * 8.0 + before
    one_hot = jnp.where((rr.astype(F32) == wanted) & (ll < 8), 1.0, 0.0).astype(BF16)
    found = sum(dot(one_hot, part, TN) for part in split3(table))
    tsel[...] = found[:8]
    vmask[...] = jnp.where(l8.astype(F32) < mine[:, 40:41], 1.0, 0.0)
    flags = jnp.where(owner_col == me_dp.astype(F32), 1.0, 0.0)
    flags = jnp.broadcast_to(flags, (readers, 128))
    lower = lax.broadcasted_iota(jnp.int32, (readers, readers), 0) > lax.broadcasted_iota(
        jnp.int32, (readers, readers), 1
    )
    place = dot(jnp.where(lower, 1.0, 0.0).astype(BF16), flags.astype(BF16))
    pick[...] = jnp.where((flags > 0.5) & (place == ll.astype(F32)), 1.0, 0.0).astype(BF16)

    for e in wcs:
        e.wait_all_recv()

    def tap_weight(q):
        return W[...].reshape(3 * C, C)[q * C : (q + 1) * C]

    act_even, act_odd = act[:rows], act[rows:]
    later = dot(act_even, tap_weight(2))
    v[...] = dot(act_even, tap_weight(0)) + dot(act_odd, tap_weight(1)) + pltpu.roll(later, rows - 1, 0)

    g2, s2 = g2_ref[...], s2_ref[...]
    eye = lax.broadcasted_iota(jnp.int32, (40, 128), 0) == lax.broadcasted_iota(jnp.int32, (40, 128), 1)

    def head_row(k, carry):
        gain_sum, shift_sum, misfit_sum, count = carry
        at = pl.ds(pl.multiple_of(k * 40, 8), 40)
        target = jnp.sum(jnp.where(eye, tsel[pl.ds(k, 1), :], 0.0), axis=1, keepdims=True)
        mask = jnp.sum(jnp.where(eye, vmask[pl.ds(k, 1), :], 0.0), axis=1, keepdims=True)
        pre = v[at, :]
        centered = pre - jnp.mean(pre, axis=1, keepdims=True)
        inv = lax.rsqrt(jnp.mean(centered * centered, axis=1, keepdims=True) + EPS)
        normed = centered * inv
        value, slope = gelu_parts(normed * g2 + s2)
        centered = value - jnp.mean(value, axis=1, keepdims=True)
        spread = jnp.mean(centered * centered, axis=1, keepdims=True) + EPS
        raw = jnp.log(spread)
        misfit = raw - target
        LG[z, x, c, pl.ds(k, 1), :] = jnp.sum(jnp.where(eye, raw * mask, 0.0), axis=0, keepdims=True)
        du = centered * (mask * misfit * (4.0 / C) / spread) * slope
        dx = du * g2
        m1 = jnp.mean(dx, axis=1, keepdims=True)
        m2 = jnp.mean(dx * normed, axis=1, keepdims=True)
        gf[at, :] = inv * (dx - m1 - normed * m2)
        return (
            gain_sum + fold8(du * normed),
            shift_sum + fold8(du),
            misfit_sum + mask * misfit * misfit,
            count + mask,
        )

    zero = jnp.zeros((8, C), F32)
    column = jnp.zeros((40, 1), F32)
    gain_sum2, shift_sum2, misfit_sum, count = lax.fori_loop(0, 8, head_row, (zero, zero, column, column), unroll=2)
    lz = Exchange("z", Z, z, lambda p: LG.at[z, x, c], lambda s: LG.at[s, x, c], (lz_s, lz_r))
    lz.start()
    grad = gf[...]
    grad_late = pltpu.roll(grad, 1, 0)
    for h in range(2):
        G[h, 0] = grad[:, 256 * h : 256 * (h + 1)].astype(BF16)
        G[h, 1] = grad_late[:, 256 * h : 256 * (h + 1)].astype(BF16)
    g_send = core_copy(2, G.at[other], lambda s: g_peer)
    g_send.start()

    def column_grads(acts, grads):
        e, o = acts[:rows], acts[rows:]
        return dot(e, grads[0], TN), dot(o, grads[0], TN), dot(e, grads[1], TN)

    own = column_grads(act, G.at[c])
    lx = Exchange("x", X, x, lambda p: LG.at[:, x, c], lambda s: LG.at[:, s, c], (lx_s, lx_r))
    lc = core_copy(3, LG.at[:, :, c], lambda s: LG.at[:, :, s])
    act_send.wait_all_recv()
    g_send.wait_all_recv()
    peers = column_grads(act_peer, g_peer)
    total = jnp.concatenate([a + b for a, b in zip(own, peers)], axis=0)
    DA[...] = total[:, :128].reshape(Y, RY, 128)
    DB[...] = total[:, 128:].reshape(Y, Z, RZ, 128).transpose(1, 0, 2, 3).reshape(Z, Y * RZ, 128)
    for full, coded in ((DA, QA), (DB, QB)):
        values = full[...]
        n, height, width = values.shape
        top = jnp.max(jnp.abs(values).reshape(n * height, width), axis=0, keepdims=True)
        power = jnp.ceil(jnp.log(jnp.maximum(top, 1e-30)) * LOG2E + 0.01) - 15.0
        ratio = jnp.exp(power * -LN2)
        coded[:, :height] = jnp.round(values * ratio[None]).astype(jnp.int32).astype(jnp.int16)
        code = jnp.broadcast_to(power, (16, width)).astype(jnp.int32).astype(jnp.int16)
        for k in range(n):
            coded[k, height:] = code

    def decoded(slot):
        height = slot.shape[0] - 16
        power = slot[height:, :].astype(jnp.int32).astype(F32)[0:1]
        return slot[:height, :].astype(jnp.int32).astype(F32) * jnp.exp(power * LN2)

    ya = Exchange("y", Y, y, lambda p: QA.at[p], lambda s: RA.at[s], (a_s, a_r))
    zb = Exchange("z", Z, z, lambda p: QB.at[p], lambda s: RB.at[s], (b_s, b_r))
    ya.start()
    zb.start()
    lz.wait_all_recv()
    lx.start()

    def whole_grad(k):
        return jnp.concatenate([G[0, k], G[1, k]], axis=1)

    now, late = whole_grad(0), whole_grad(1)
    dact[:rows] = dot(now, tap_weight(0), NT) + dot(late, tap_weight(2), NT)
    dact[rows:] = dot(now, tap_weight(1), NT)

    def backward_chunk(i, carry):
        gain_sum, shift_sum = carry
        at = pl.ds(pl.multiple_of(i * CHUNK, CHUNK), CHUNK)
        normed = xh[at, :]
        du = dact[at, :] * dg[at, :]
        dx = du * g1
        m1 = jnp.mean(dx, axis=1, keepdims=True)
        m2 = jnp.mean(dx * normed, axis=1, keepdims=True)
        dpre = rs[at, :1] * (dx - m1 - normed * m2)
        hi, mid = split2(dpre)
        gph[at, :] = hi
        gpm[at, :] = mid
        return gain_sum + fold8(du * normed), shift_sum + fold8(du)

    gain_sum1, shift_sum1 = lax.fori_loop(0, chunks, backward_chunk, (zero, zero), unroll=2)
    taps = dot(xcol[...], gph[...], TN) + dot(xcol[...], gpm[...], TN)
    ri = lax.broadcasted_iota(jnp.int32, (8, C), 0)
    li = lax.broadcasted_iota(jnp.int32, (8, C), 1)

    def line(vector, k):
        return jnp.where(ri == k, jnp.sum(vector, axis=0, keepdims=True), 0.0)

    loss_line = jnp.where(
        li == 0,
        jnp.sum(misfit_sum, axis=0, keepdims=True),
        jnp.where(li == 1, jnp.sum(count, axis=0, keepdims=True), 0.0),
    )
    groups = [
        taps[0:8] + taps[8:16],
        taps[32:40] + taps[40:48],
        line(gain_sum1, 0) + line(shift_sum1, 1) + line(gain_sum2, 2) + line(shift_sum2, 3)
        + jnp.where(ri == 4, loss_line, 0.0),
        zero,
    ]
    for i, group in enumerate(groups):
        for j in range(4):
            S[i // 2, 4 * (i % 2) + j] = group[:, 128 * j : 128 * (j + 1)]
    sc = core_copy(4, S.at[other], lambda s: S_peer)
    sc.start()
    lx.wait_all_recv()
    lc.start()
    sc.wait_all_recv()
    S1[...] = (S[c] + S_peer[...]).reshape(Y, per_y, 8, 128)
    sy = Exchange("y", Y, y, lambda p: S1.at[p], lambda s: SY.at[s], (sy_s, sy_r))
    sy.start()

    total = DA[y]
    for r in range(1, Y):
        ya.wait_recv(r)
        total = total + decoded(RA.at[ya.sender(r)])
    A1[...] = total.reshape(Z, RZ, 128)
    za = Exchange("z", Z, z, lambda p: A1.at[p], lambda s: RA2.at[s], (a2_s, a2_r))
    za.start()
    total = DB[z]
    for r in range(1, Z):
        zb.wait_recv(r)
        total = total + decoded(RB.at[zb.sender(r)])
    B1[...] = total.reshape(Y, RZ, 128)
    yb = Exchange("y", Y, y, lambda p: B1.at[p], lambda s: RB2.at[s], (b2_s, b2_r))
    yb.start()
    sy.wait_all_recv()
    SY[y] = S1[y]
    total = SY[0]
    for k in range(1, Y):
        total = total + SY[k]
    SZ[z] = total
    sz = Exchange("z", Z, z, lambda p: SZ.at[z], lambda s: SZ.at[s], (sz_s, sz_r))
    sz.start()

    first = A1[z]
    for r in range(1, Z):
        za.wait_recv(r)
        first = first + RA2[za.sender(r)]
    second = B1[y]
    for r in range(1, Y):
        yb.wait_recv(r)
        second = second + RB2[yb.sender(r)]
    XR[x] = jnp.concatenate([first, second], axis=1)
    xs = Exchange("x", X, x, lambda p: XR.at[x], lambda s: XR.at[s], (x_s, x_r))
    xs.start()
    sz.wait_all_recv()
    total = SZ[0]
    for k in range(1, Z):
        total = total + SZ[k]
    SX[x] = total
    sx = Exchange("x", X, x, lambda p: SX.at[x], lambda s: SX.at[s], (sx_s, sx_r))
    sx.start()

    def rows_of(k):
        return pl.ds(pl.multiple_of(k * RZ, 8), RZ)

    xs.wait_all_recv()
    total = XR[0]
    for k in range(1, X):
        total = total + XR[k]
    gw2_ref[rows_of(z), half] = total
    zg = Exchange(
        "z", Z, z, lambda p: gw2_ref.at[rows_of(z), half], lambda s: gw2_ref.at[rows_of(s), half], (z_s, z_r)
    )
    zg.start()
    sx.wait_all_recv()
    total = SX[0]
    for k in range(1, X):
        total = total + SX[k]
    SA[y] = total
    sa = Exchange("y", Y, y, lambda p: SA.at[y], lambda s: SA.at[s], (sa_s, sa_r))
    sa.start()

    lc.wait_all_recv()
    logs = LG[...].reshape(readers, 128)
    picked = sum(dot(pick[...], part, TN) for part in split3(logs))
    lv_ref[...] = picked[:8, : lv_ref.shape[1]]

    zg.wait_all_recv()
    fin = core_copy(5, gw2_ref.at[:, half], lambda s: gw2_ref.at[:, half_of(s)])
    fin.start()

    sa.wait_all_recv()
    small_ref[c] = SA[...].reshape(TILES // 2, 8, 128)
    sf = core_copy(6, small_ref.at[c], lambda s: small_ref.at[s])
    sf.start()
    sf.wait_all_recv()
    fin.wait_all_recv()

    waiting = [wy, tc, tx, tz, act_send, g_send, lc, lx, lz, ya, zb, za, yb, xs, zg, sc, sy, sz, sx, sa, sf, fin]
    for e in waiting + wxs + wcs:
        e.wait_sends()


def write_kernel(lv_in, gw2_in, small, lv_ref, loss_ref, gw2_ref, gw1_ref, gg1_ref, gs1_ref, gg2_ref, gs2_ref):
    def wide(i):
        return jnp.concatenate([small[i // 2, 4 * (i % 2) + j] for j in range(4)], axis=1)

    lv_ref[...] = lv_in[...]
    gw2_ref[...] = gw2_in[...]
    gw1_ref[0:5] = wide(0)[0:5]
    gw1_ref[5:10] = wide(1)[0:5]
    norms = wide(2)
    gg1_ref[...] = norms[0:1]
    gs1_ref[...] = norms[1:2]
    gg2_ref[...] = norms[2:3]
    gs2_ref[...] = norms[3:4]
    loss_ref[...] = norms[4:5, 0:1] / norms[4:5, 1:2]


def per_device(sizes, waveform, lengths, owner_of, targets, first_weight, first_gain, first_shift,
               second_weight, second_gain, second_shift):
    Z, X, Y = sizes
    row_total, later = targets.shape
    RY = second_weight.shape[0]
    RZ = RY // Z
    rows = 320
    dma = pltpu.SemaphoreType.DMA
    vm = pltpu.VMEM
    per_y = TILES // 2 // Y
    scratch = [
        vm((Y, RY, C), BF16), vm((Z, X, 2, 8, 128), F32), vm((Z, X, 2, 8, 128), F32), vm((8, 128), F32),
        vm((8, 512), F32), vm((128, C), F32), vm((2 * rows, 128), BF16),
        vm((2 * rows, C), F32), vm((2 * rows, C), F32), vm((2 * rows, 128), F32),
        vm((2 * rows, C), BF16), vm((2 * rows, C), BF16), vm((rows, C), F32),
        vm((8, 128), F32), vm((8, 128), F32), vm((rows, C), F32),
        vm((2, 2, rows, 256), BF16), vm((2, rows, 256), BF16),
        vm((Y, RY, 128), F32), vm((Z, Y * RZ, 128), F32),
        vm((Y, RY + 16, 128), jnp.int16), vm((Z, Y * RZ + 16, 128), jnp.int16),
        vm((Y, RY + 16, 128), jnp.int16), vm((Z, Y * RZ + 16, 128), jnp.int16),
        vm((Z, RZ, 128), F32), vm((Y, RZ, 128), F32), vm((Z, RZ, 128), F32), vm((Y, RZ, 128), F32),
        vm((X, RZ, 256), F32), vm((2 * rows, C), F32), vm((2 * rows, C), BF16), vm((2 * rows, C), BF16),
        vm((2, TILES // 2, 8, 128), F32), vm((TILES // 2, 8, 128), F32), vm((Y, per_y, 8, 128), F32),
        vm((Y, per_y, 8, 128), F32), vm((Z, per_y, 8, 128), F32), vm((X, per_y, 8, 128), F32),
        vm((Y, per_y, 8, 128), F32), vm((Z * X * 2 * 8, 128), BF16),
        dma((Y,)), dma((Y,)), dma((Y, X)), dma((Y, X)), dma((Y, 2)), dma((Y, 2)),
        dma((X,)), dma((X,)), dma((Z,)), dma((Z,)), dma((X,)), dma((X,)), dma((Z,)), dma((Z,)),
        dma((Y,)), dma((Y,)), dma((Z,)), dma((Z,)), dma((Z,)), dma((Z,)), dma((Y,)), dma((Y,)),
        dma((X,)), dma((X,)), dma((Z,)), dma((Z,)),
        dma((Y,)), dma((Y,)), dma((Z,)), dma((Z,)), dma((X,)), dma((X,)), dma((Y,)), dma((Y,)),
        dma((8, 2)), dma((8, 2)),
    ]
    shapes = [
        (row_total, later), (1, 1), (RY, C), (10, C), (1, C), (1, C), (1, C), (1, C),
    ]
    whole = pl.BlockSpec(memory_space=pltpu.VMEM)
    scalars = pl.BlockSpec(memory_space=pltpu.SMEM)
    sums = pl.pallas_call(
        functools.partial(kernel, sizes),
        out_shape=[jax.ShapeDtypeStruct(s, F32) for s in (shapes[0], shapes[2], (2, TILES // 2, 8, 128))],
        in_specs=[whole, whole, scalars, scalars] + [whole] * 6,
        out_specs=[whole] * 3,
        scratch_shapes=scratch,
        compiler_params=pltpu.CompilerParams(
            collective_id=0, has_side_effects=True, vmem_limit_bytes=56 * 2**20
        ),
    )(
        waveform, targets, owner_of, lengths, first_weight, first_gain[None], first_shift[None],
        second_weight, second_gain[None], second_shift[None],
    )
    out = pl.pallas_call(
        write_kernel,
        out_shape=[jax.ShapeDtypeStruct(s, F32) for s in shapes],
        in_specs=[whole] * 3,
        out_specs=[whole] * len(shapes),
    )(*sums)
    lv, loss, gw2, gw1, gg1, gs1, gg2, gs2 = out
    return lv, loss[0, 0], gw2, gw1, gg1[0], gs1[0], gg2[0], gs2[0]


def solution(mesh):
    dp, fsdp = mesh.shape["dp"], mesh.shape["fsdp"]
    x = 4 if dp >= 64 else 2
    z = dp // (2 * x)
    torus = Mesh(mesh.devices.reshape(z, x, 2, fsdp), ("dp_0", "dp_1", "dp_2", "fsdp"))
    return jax.shard_map(
        functools.partial(per_device, (z, x, fsdp)),
        mesh=torus,
        in_specs=(
            P(DP_FSDP, None), P(DP_FSDP), P(DP_FSDP), P(DP_FSDP, None), P(), P(), P(),
            P("fsdp", None), P(), P(),
        ),
        out_specs=(P(DP_FSDP, None), P(), P("fsdp", None), P(), P(), P(), P(), P()),
        check_vma=False,
    )
```

```python
import functools

import jax
import jax.numpy as jnp
from jax import lax
from jax.experimental import pallas as pl
from jax.experimental.pallas import tpu as pltpu
from jax.sharding import Mesh
from jax.sharding import PartitionSpec as P

DP = ("dp_0", "dp_1", "dp_2")
DP_FSDP = ("dp_0", "dp_1", "dp_2", "fsdp")
AXES = {"z": "dp_0", "x": "dp_1", "c": "dp_2", "y": "fsdp"}
EPS = 1e-05
C = 512
F32 = jnp.float32
BF16 = jnp.bfloat16
MESH = pl.DeviceIdType.MESH
TN = (((0,), (0,)), ((), ()))
NT = (((1,), (1,)), ((), ()))
TILES = 16
CHUNK = 32
LN2 = 0.6931471805599453
LOG2E = 1.4426950408889634


class Exchange:
    def __init__(self, axis, size, me, src, dst, sems):
        self.axis, self.size, self.me = axis, size, me
        self.src, self.dst = src, dst
        self.send_sems, self.recv_sems = sems

    def _copy(self, r, slot, peer):
        return pltpu.make_async_remote_copy(
            src_ref=self.src(peer),
            dst_ref=self.dst(slot),
            send_sem=self.send_sems.at[r],
            recv_sem=self.recv_sems.at[r],
            device_id={AXES[self.axis]: peer},
            device_id_type=MESH,
        )

    def start(self):
        for r in sorted(range(1, self.size), key=lambda r: -min(r, self.size - r)):
            self._copy(r, self.me, lax.rem(self.me + r, self.size)).start()

    def sender(self, r):
        return lax.rem(self.me + self.size - r, self.size)

    def wait_recv(self, r):
        s = self.sender(r)
        self._copy(r, s, s).wait_recv()

    def wait_all_recv(self):
        for r in range(1, self.size):
            self.wait_recv(r)

    def wait_sends(self):
        for r in range(1, self.size):
            self._copy(r, self.me, lax.rem(self.me + r, self.size)).wait_send()


def dot(a, b, dims=(((1,), (0,)), ((), ()))):
    return lax.dot_general(a, b, dims, preferred_element_type=F32)


def split2(v):
    hi = v.astype(BF16)
    return hi, (v - hi.astype(F32)).astype(BF16)


def split3(v):
    hi, mid = split2(v)
    return hi, mid, (v - hi.astype(F32) - mid.astype(F32)).astype(BF16)


def gelu_parts(u):
    a = jnp.abs(u)
    t = 1.0 / (1.0 + 0.23164190 * a)
    e = jnp.exp(u * u * -0.5)
    poly = 0.5 * 1.061405429
    poly = poly * t - 0.5 * 1.453152027
    poly = poly * t + 0.5 * 1.421413741
    poly = poly * t - 0.5 * 0.284496736
    poly = poly * t + 0.5 * 0.254829592
    tail = poly * t * e
    cdf = jnp.where(u >= 0.0, 1.0 - tail, tail)
    return u * cdf, cdf + u * (e * 0.3989422804014327)


def fold8(v):
    return v.reshape(v.shape[0] // 8, 8, v.shape[1]).sum(axis=0)


def kernel(sizes, *refs):
    Z, X, Y = sizes
    (wave_ref, tgt_ref, own_ref, len_ref, fw_ref, g1_ref, s1_ref, w_ref, g2_ref, s2_ref,
     lv_ref, gw2_ref, small_ref,
     W, TG, LG, blk, wpad, wconv, xcol, xh, dg, rs, act, act_peer, v, tsel, vmask, gf, G, g_peer,
     DA, DB, QA, QB, RA, RB, A1, B1, RA2, RB2, XR, dact, gph, gpm, S, S_peer, SY, S1, SZ, SX, SA, pick,
     w_sy, w_ry, w_sd, w_rd, w_sx, w_rx, w_sc, w_rc, tx_s, tx_r, tz_s, tz_r, lx_s, lx_r, lz_s, lz_r,
     a_s, a_r, b_s, b_r, a2_s, a2_r, b2_s, b2_r, x_s, x_r, z_s, z_r,
     sy_s, sy_r, sz_s, sz_r, sx_s, sx_r, sa_s, sa_r, c_s, c_r) = refs
    z, x, c, y = (lax.axis_index(AXES[k]) for k in "zxcy")
    other = 1 - c
    RY = W.shape[1]
    routed = RY // 2
    halves = X // 2
    RX = routed // halves
    RZ = RY // Z
    rows = 8 * 40
    per_y = TILES // 2 // Y
    dp = Z * X * 2
    readers = dp * 8
    me_dp = (z * X + x) * 2 + c

    barrier = pltpu.get_barrier_semaphore()
    for axis, size, me in (("c", 2, c), ("x", X, x), ("y", Y, y), ("z", Z, z)):
        for r in range(1, size):
            pl.semaphore_signal(
                barrier, inc=1, device_id={AXES[axis]: lax.rem(me + r, size)}, device_id_type=MESH
            )

    def core_copy(k, src, dst):
        return Exchange("c", 2, c, lambda p: src, dst, (c_s.at[k], c_r.at[k]))

    half = pl.ds(pl.multiple_of(c * 256, 256), 256)

    W[y] = w_ref[...]
    r8 = lax.broadcasted_iota(jnp.int32, (8, 128), 0)
    l8 = lax.broadcasted_iota(jnp.int32, (8, 128), 1)
    numbers = jnp.zeros((8, 128), jnp.int32)
    for k in range(8):
        valid = ((len_ref[k] - 10) // 5 - 2) // 2 + 1
        numbers = jnp.where(r8 == k, jnp.where(l8 == 39, own_ref[k], valid), numbers)
    blk[...] = numbers.astype(F32)
    blk[:, : tgt_ref.shape[1]] = tgt_ref[...]
    TG[z, x, c] = blk[...]

    def part_rows(k):
        return pl.ds(pl.multiple_of(k % halves * RX, 16), RX)

    def part_lanes(k):
        return pl.ds(pl.multiple_of(c * 256 + k // halves * 128, 128), 128)

    pl.semaphore_wait(barrier, 1 + (X - 1) + (Y - 1) + (Z - 1))

    wy = Exchange(
        "y", Y, y, lambda p: W.at[y, part_rows(x), part_lanes(x)],
        lambda s: W.at[s, part_rows(x), part_lanes(x)], (w_sy, w_ry),
    )
    wy.start()
    rest = pl.ds(routed, RY - routed)
    wd = Exchange("y", Y, y, lambda p: W.at[y, rest, half], lambda s: W.at[s, rest, half], (w_sd, w_rd))

    def wx(k, slot):
        return Exchange(
            "x", X, x, lambda p: W.at[slot, part_rows(x), part_lanes(x)],
            lambda s: W.at[slot, part_rows(s), part_lanes(s)], (w_sx.at[k], w_rx.at[k]),
        )

    def half_of(k):
        return pl.ds(pl.multiple_of(k * 256, 256), 256)

    def wc(k, slot):
        return Exchange(
            "c", 2, c, lambda p: W.at[slot, :, half], lambda s: W.at[slot, :, half_of(s)],
            (w_sc.at[k], w_rc.at[k]),
        )

    wxs = [wx(r, wy.sender(r)) for r in range(1, Y)]
    wcs = [wc(r, wy.sender(r)) for r in range(1, Y)]
    tz = Exchange("z", Z, z, lambda p: TG.at[z, x, c], lambda s: TG.at[s, x, c], (tz_s, tz_r))
    tz.start()
    tx = Exchange("x", X, x, lambda p: TG.at[:, x, c], lambda s: TG.at[:, s, c], (tx_s, tx_r))
    tc = core_copy(0, TG.at[:, :, c], lambda s: TG.at[:, :, s])

    wpad[...] = jnp.zeros_like(wpad)
    wpad[:, : wave_ref.shape[1]] = wave_ref[...]
    samples = lax.broadcasted_iota(jnp.int32, (512, 128), 0).astype(F32)
    lanes = lax.broadcasted_iota(jnp.int32, (512, 128), 1).astype(F32)
    tap = samples - 5.0 * jnp.floor((samples + 0.5) * 0.2)
    place_hi = jnp.where((lanes == tap) | (lanes == tap + 16.0), 1.0, 0.0).astype(BF16)
    place_mid = jnp.where(lanes == tap + 8.0, 1.0, 0.0).astype(BF16)
    frame = lax.broadcasted_iota(jnp.int32, (40, 512), 0)
    offset = lax.broadcasted_iota(jnp.int32, (40, 512), 1) - 10 * frame
    in_even = (offset >= 0) & (offset < 5)
    in_odd = (offset >= 5) & (offset < 10)
    even, odd = [], []
    for k in range(8):
        row = jnp.broadcast_to(wpad[k : k + 1, :], (40, 512))
        even.append(jnp.where(in_even, row, 0.0))
        odd.append(jnp.where(in_odd, row, 0.0))
    blocks = []
    for parts in (even, odd):
        hi, mid = split2(jnp.concatenate(parts, axis=0))
        blocks.append(dot(hi, place_hi) + dot(mid, place_mid))
    even_block, odd_block = blocks
    xcol[:rows] = (even_block + pltpu.roll(odd_block, 32, 1)).astype(BF16)
    xcol[rows:] = (odd_block + pltpu.roll(pltpu.roll(even_block, rows - 1, 0), 32, 1)).astype(BF16)
    wconv[...] = jnp.zeros_like(wconv)
    fw = fw_ref[...]
    fw_hi = fw.astype(BF16).astype(F32)
    fw_mid = (fw - fw_hi).astype(BF16).astype(F32)
    for base, taps in ((0, slice(0, 5)), (32, slice(5, 10))):
        wconv[base : base + 5] = fw_hi[taps]
        wconv[base + 8 : base + 13] = fw_hi[taps]
        wconv[base + 16 : base + 21] = fw_mid[taps]
    xh[...] = dot(xcol[...], wconv[...].astype(BF16))

    wd.start()
    g1, s1 = g1_ref[...], s1_ref[...]

    def forward_chunk(i, carry):
        at = pl.ds(pl.multiple_of(i * CHUNK, CHUNK), CHUNK)
        pre = xh[at, :]
        centered = pre - jnp.mean(pre, axis=1, keepdims=True)
        inv = lax.rsqrt(jnp.mean(centered * centered, axis=1, keepdims=True) + EPS)
        normed = centered * inv
        value, slope = gelu_parts(normed * g1 + s1)
        xh[at, :] = normed
        dg[at, :] = slope
        rs[at, :] = jnp.broadcast_to(inv, (CHUNK, 128))
        act[at, :] = value.astype(BF16)
        return carry

    chunks = 2 * rows // CHUNK
    near_first = sorted(range(1, Y), key=lambda r: min(r, Y - r))
    steps = 4
    for k in range(steps):
        for r in near_first[k * 2 : (k + 1) * 2 if k < 2 else Y] if k < 3 else ():
            wy.wait_recv(r)
            wxs[r - 1].start()
        if k == 1:
            tz.wait_all_recv()
            tx.start()
        if k == 3:
            tx.wait_all_recv()
            tc.start()
        lax.fori_loop(chunks * k // steps, chunks * (k + 1) // steps, forward_chunk, 0, unroll=True)
    act_send = core_copy(1, act, lambda s: act_peer)
    act_send.start()
    for r in near_first:
        wxs[r - 1].wait_all_recv()
        wd.wait_recv(r)
        wcs[r - 1].start()

    tc.wait_all_recv()
    table = TG[...].reshape(readers, 128)
    owner_col = table[:, 39:40]
    mine = blk[...]
    owner_row = jnp.sum(jnp.where(r8 == l8, mine[:, 39:40], 0.0), axis=0, keepdims=True)
    rr = lax.broadcasted_iota(jnp.int32, (readers, 128), 0)
    ll = lax.broadcasted_iota(jnp.int32, (readers, 128), 1)
    before = jnp.sum(
        jnp.where((owner_col == owner_row) & (rr < me_dp * 8), 1.0, 0.0), axis=0, keepdims=True
    )
    wanted = owner_row * 8.0 + before
    one_hot = jnp.where((rr.astype(F32) == wanted) & (ll < 8), 1.0, 0.0).astype(BF16)
    found = sum(dot(one_hot, part, TN) for part in split3(table))
    tsel[...] = found[:8]
    vmask[...] = jnp.where(l8.astype(F32) < mine[:, 40:41], 1.0, 0.0)
    flags = jnp.where(owner_col == me_dp.astype(F32), 1.0, 0.0)
    flags = jnp.broadcast_to(flags, (readers, 128))
    lower = lax.broadcasted_iota(jnp.int32, (readers, readers), 0) > lax.broadcasted_iota(
        jnp.int32, (readers, readers), 1
    )
    place = dot(jnp.where(lower, 1.0, 0.0).astype(BF16), flags.astype(BF16))
    pick[...] = jnp.where((flags > 0.5) & (place == ll.astype(F32)), 1.0, 0.0).astype(BF16)

    for e in wcs:
        e.wait_all_recv()

    def tap_weight(q):
        return W[...].reshape(3 * C, C)[q * C : (q + 1) * C]

    act_even, act_odd = act[:rows], act[rows:]
    later = dot(act_even, tap_weight(2))
    v[...] = dot(act_even, tap_weight(0)) + dot(act_odd, tap_weight(1)) + pltpu.roll(later, rows - 1, 0)

    g2, s2 = g2_ref[...], s2_ref[...]
    eye = lax.broadcasted_iota(jnp.int32, (40, 128), 0) == lax.broadcasted_iota(jnp.int32, (40, 128), 1)

    def head_row(k, carry):
        gain_sum, shift_sum, misfit_sum, count = carry
        at = pl.ds(pl.multiple_of(k * 40, 8), 40)
        target = jnp.sum(jnp.where(eye, tsel[pl.ds(k, 1), :], 0.0), axis=1, keepdims=True)
        mask = jnp.sum(jnp.where(eye, vmask[pl.ds(k, 1), :], 0.0), axis=1, keepdims=True)
        pre = v[at, :]
        centered = pre - jnp.mean(pre, axis=1, keepdims=True)
        inv = lax.rsqrt(jnp.mean(centered * centered, axis=1, keepdims=True) + EPS)
        normed = centered * inv
        value, slope = gelu_parts(normed * g2 + s2)
        centered = value - jnp.mean(value, axis=1, keepdims=True)
        spread = jnp.mean(centered * centered, axis=1, keepdims=True) + EPS
        raw = jnp.log(spread)
        misfit = raw - target
        LG[z, x, c, pl.ds(k, 1), :] = jnp.sum(jnp.where(eye, raw * mask, 0.0), axis=0, keepdims=True)
        du = centered * (mask * misfit * (4.0 / C) / spread) * slope
        dx = du * g2
        m1 = jnp.mean(dx, axis=1, keepdims=True)
        m2 = jnp.mean(dx * normed, axis=1, keepdims=True)
        gf[at, :] = inv * (dx - m1 - normed * m2)
        return (
            gain_sum + fold8(du * normed),
            shift_sum + fold8(du),
            misfit_sum + mask * misfit * misfit,
            count + mask,
        )

    zero = jnp.zeros((8, C), F32)
    column = jnp.zeros((40, 1), F32)
    gain_sum2, shift_sum2, misfit_sum, count = lax.fori_loop(0, 8, head_row, (zero, zero, column, column), unroll=4)
    lz = Exchange("z", Z, z, lambda p: LG.at[z, x, c], lambda s: LG.at[s, x, c], (lz_s, lz_r))
    lz.start()
    grad = gf[...]
    grad_late = pltpu.roll(grad, 1, 0)
    for h in range(2):
        G[h, 0] = grad[:, 256 * h : 256 * (h + 1)].astype(BF16)
        G[h, 1] = grad_late[:, 256 * h : 256 * (h + 1)].astype(BF16)
    g_send = core_copy(2, G.at[other], lambda s: g_peer)
    g_send.start()

    def column_grads(acts, grads):
        e, o = acts[:rows], acts[rows:]
        return dot(e, grads[0], TN), dot(o, grads[0], TN), dot(e, grads[1], TN)

    own = column_grads(act, G.at[c])
    lx = Exchange("x", X, x, lambda p: LG.at[:, x, c], lambda s: LG.at[:, s, c], (lx_s, lx_r))
    lc = core_copy(3, LG.at[:, :, c], lambda s: LG.at[:, :, s])
    act_send.wait_all_recv()
    g_send.wait_all_recv()
    peers = column_grads(act_peer, g_peer)
    total = jnp.concatenate([a + b for a, b in zip(own, peers)], axis=0)
    DA[...] = total[:, :128].reshape(Y, RY, 128)
    DB[...] = total[:, 128:].reshape(Y, Z, RZ, 128).transpose(1, 0, 2, 3).reshape(Z, Y * RZ, 128)
    for full, coded in ((DA, QA), (DB, QB)):
        values = full[...]
        n, height, width = values.shape
        top = jnp.max(jnp.abs(values).reshape(n * height, width), axis=0, keepdims=True)
        power = jnp.ceil(jnp.log(jnp.maximum(top, 1e-30)) * LOG2E + 0.01) - 15.0
        ratio = jnp.exp(power * -LN2)
        coded[:, :height] = jnp.round(values * ratio[None]).astype(jnp.int32).astype(jnp.int16)
        code = jnp.broadcast_to(power, (16, width)).astype(jnp.int32).astype(jnp.int16)
        for k in range(n):
            coded[k, height:] = code

    def decoded(slot):
        height = slot.shape[0] - 16
        power = slot[height:, :].astype(jnp.int32).astype(F32)[0:1]
        return slot[:height, :].astype(jnp.int32).astype(F32) * jnp.exp(power * LN2)

    ya = Exchange("y", Y, y, lambda p: QA.at[p], lambda s: RA.at[s], (a_s, a_r))
    zb = Exchange("z", Z, z, lambda p: QB.at[p], lambda s: RB.at[s], (b_s, b_r))
    ya.start()
    zb.start()
    lz.wait_all_recv()
    lx.start()

    def whole_grad(k):
        return jnp.concatenate([G[0, k], G[1, k]], axis=1)

    now, late = whole_grad(0), whole_grad(1)
    dact[:rows] = dot(now, tap_weight(0), NT) + dot(late, tap_weight(2), NT)
    dact[rows:] = dot(now, tap_weight(1), NT)

    def backward_chunk(i, carry):
        gain_sum, shift_sum = carry
        at = pl.ds(pl.multiple_of(i * CHUNK, CHUNK), CHUNK)
        normed = xh[at, :]
        du = dact[at, :] * dg[at, :]
        dx = du * g1
        m1 = jnp.mean(dx, axis=1, keepdims=True)
        m2 = jnp.mean(dx * normed, axis=1, keepdims=True)
        dpre = rs[at, :1] * (dx - m1 - normed * m2)
        hi, mid = split2(dpre)
        gph[at, :] = hi
        gpm[at, :] = mid
        return gain_sum + fold8(du * normed), shift_sum + fold8(du)

    gain_sum1, shift_sum1 = lax.fori_loop(0, chunks, backward_chunk, (zero, zero), unroll=2)
    taps = dot(xcol[...], gph[...], TN) + dot(xcol[...], gpm[...], TN)
    ri = lax.broadcasted_iota(jnp.int32, (8, C), 0)
    li = lax.broadcasted_iota(jnp.int32, (8, C), 1)

    def line(vector, k):
        return jnp.where(ri == k, jnp.sum(vector, axis=0, keepdims=True), 0.0)

    loss_line = jnp.where(
        li == 0,
        jnp.sum(misfit_sum, axis=0, keepdims=True),
        jnp.where(li == 1, jnp.sum(count, axis=0, keepdims=True), 0.0),
    )
    groups = [
        taps[0:8] + taps[8:16],
        taps[32:40] + taps[40:48],
        line(gain_sum1, 0) + line(shift_sum1, 1) + line(gain_sum2, 2) + line(shift_sum2, 3)
        + jnp.where(ri == 4, loss_line, 0.0),
        zero,
    ]
    for i, group in enumerate(groups):
        for j in range(4):
            S[i // 2, 4 * (i % 2) + j] = group[:, 128 * j : 128 * (j + 1)]
    sc = core_copy(4, S.at[other], lambda s: S_peer)
    sc.start()
    lx.wait_all_recv()
    lc.start()
    sc.wait_all_recv()
    S1[...] = (S[c] + S_peer[...]).reshape(Y, per_y, 8, 128)
    sy = Exchange("y", Y, y, lambda p: S1.at[p], lambda s: SY.at[s], (sy_s, sy_r))
    sy.start()

    total = DA[y]
    for r in range(1, Y):
        ya.wait_recv(r)
        total = total + decoded(RA.at[ya.sender(r)])
    A1[...] = total.reshape(Z, RZ, 128)
    za = Exchange("z", Z, z, lambda p: A1.at[p], lambda s: RA2.at[s], (a2_s, a2_r))
    za.start()
    total = DB[z]
    for r in range(1, Z):
        zb.wait_recv(r)
        total = total + decoded(RB.at[zb.sender(r)])
    B1[...] = total.reshape(Y, RZ, 128)
    yb = Exchange("y", Y, y, lambda p: B1.at[p], lambda s: RB2.at[s], (b2_s, b2_r))
    yb.start()
    sy.wait_all_recv()
    SY[y] = S1[y]
    total = SY[0]
    for k in range(1, Y):
        total = total + SY[k]
    SZ[z] = total
    sz = Exchange("z", Z, z, lambda p: SZ.at[z], lambda s: SZ.at[s], (sz_s, sz_r))
    sz.start()

    first = A1[z]
    for r in range(1, Z):
        za.wait_recv(r)
        first = first + RA2[za.sender(r)]
    second = B1[y]
    for r in range(1, Y):
        yb.wait_recv(r)
        second = second + RB2[yb.sender(r)]
    XR[x] = jnp.concatenate([first, second], axis=1)
    xs = Exchange("x", X, x, lambda p: XR.at[x], lambda s: XR.at[s], (x_s, x_r))
    xs.start()
    sz.wait_all_recv()
    total = SZ[0]
    for k in range(1, Z):
        total = total + SZ[k]
    SX[x] = total
    sx = Exchange("x", X, x, lambda p: SX.at[x], lambda s: SX.at[s], (sx_s, sx_r))
    sx.start()

    def rows_of(k):
        return pl.ds(pl.multiple_of(k * RZ, 8), RZ)

    xs.wait_all_recv()
    total = XR[0]
    for k in range(1, X):
        total = total + XR[k]
    gw2_ref[rows_of(z), half] = total
    zg = Exchange(
        "z", Z, z, lambda p: gw2_ref.at[rows_of(z), half], lambda s: gw2_ref.at[rows_of(s), half], (z_s, z_r)
    )
    zg.start()
    sx.wait_all_recv()
    total = SX[0]
    for k in range(1, X):
        total = total + SX[k]
    SA[y] = total
    sa = Exchange("y", Y, y, lambda p: SA.at[y], lambda s: SA.at[s], (sa_s, sa_r))
    sa.start()

    lc.wait_all_recv()
    logs = LG[...].reshape(readers, 128)
    picked = sum(dot(pick[...], part, TN) for part in split3(logs))
    lv_ref[...] = picked[:8, : lv_ref.shape[1]]

    zg.wait_all_recv()
    fin = core_copy(5, gw2_ref.at[:, half], lambda s: gw2_ref.at[:, half_of(s)])
    fin.start()

    sa.wait_all_recv()
    small_ref[c] = SA[...].reshape(TILES // 2, 8, 128)
    sf = core_copy(6, small_ref.at[c], lambda s: small_ref.at[s])
    sf.start()
    sf.wait_all_recv()
    fin.wait_all_recv()

    waiting = [wy, wd, tc, tx, tz, act_send, g_send, lc, lx, lz, ya, zb, za, yb, xs, zg, sc, sy, sz, sx, sa, sf, fin]
    for e in waiting + wxs + wcs:
        e.wait_sends()


def write_kernel(lv_in, gw2_in, small, lv_ref, loss_ref, gw2_ref, gw1_ref, gg1_ref, gs1_ref, gg2_ref, gs2_ref):
    def wide(i):
        return jnp.concatenate([small[i // 2, 4 * (i % 2) + j] for j in range(4)], axis=1)

    lv_ref[...] = lv_in[...]
    gw2_ref[...] = gw2_in[...]
    gw1_ref[0:5] = wide(0)[0:5]
    gw1_ref[5:10] = wide(1)[0:5]
    norms = wide(2)
    gg1_ref[...] = norms[0:1]
    gs1_ref[...] = norms[1:2]
    gg2_ref[...] = norms[2:3]
    gs2_ref[...] = norms[3:4]
    loss_ref[...] = norms[4:5, 0:1] / norms[4:5, 1:2]


def per_device(sizes, waveform, lengths, owner_of, targets, first_weight, first_gain, first_shift,
               second_weight, second_gain, second_shift):
    Z, X, Y = sizes
    row_total, later = targets.shape
    RY = second_weight.shape[0]
    RZ = RY // Z
    rows = 320
    dma = pltpu.SemaphoreType.DMA
    vm = pltpu.VMEM
    per_y = TILES // 2 // Y
    scratch = [
        vm((Y, RY, C), BF16), vm((Z, X, 2, 8, 128), F32), vm((Z, X, 2, 8, 128), F32), vm((8, 128), F32),
        vm((8, 512), F32), vm((128, C), F32), vm((2 * rows, 128), BF16),
        vm((2 * rows, C), F32), vm((2 * rows, C), F32), vm((2 * rows, 128), F32),
        vm((2 * rows, C), BF16), vm((2 * rows, C), BF16), vm((rows, C), F32),
        vm((8, 128), F32), vm((8, 128), F32), vm((rows, C), F32),
        vm((2, 2, rows, 256), BF16), vm((2, rows, 256), BF16),
        vm((Y, RY, 128), F32), vm((Z, Y * RZ, 128), F32),
        vm((Y, RY + 16, 128), jnp.int16), vm((Z, Y * RZ + 16, 128), jnp.int16),
        vm((Y, RY + 16, 128), jnp.int16), vm((Z, Y * RZ + 16, 128), jnp.int16),
        vm((Z, RZ, 128), F32), vm((Y, RZ, 128), F32), vm((Z, RZ, 128), F32), vm((Y, RZ, 128), F32),
        vm((X, RZ, 256), F32), vm((2 * rows, C), F32), vm((2 * rows, C), BF16), vm((2 * rows, C), BF16),
        vm((2, TILES // 2, 8, 128), F32), vm((TILES // 2, 8, 128), F32), vm((Y, per_y, 8, 128), F32),
        vm((Y, per_y, 8, 128), F32), vm((Z, per_y, 8, 128), F32), vm((X, per_y, 8, 128), F32),
        vm((Y, per_y, 8, 128), F32), vm((Z * X * 2 * 8, 128), BF16),
        dma((Y,)), dma((Y,)), dma((Y,)), dma((Y,)), dma((Y, X)), dma((Y, X)), dma((Y, 2)), dma((Y, 2)),
        dma((X,)), dma((X,)), dma((Z,)), dma((Z,)), dma((X,)), dma((X,)), dma((Z,)), dma((Z,)),
        dma((Y,)), dma((Y,)), dma((Z,)), dma((Z,)), dma((Z,)), dma((Z,)), dma((Y,)), dma((Y,)),
        dma((X,)), dma((X,)), dma((Z,)), dma((Z,)),
        dma((Y,)), dma((Y,)), dma((Z,)), dma((Z,)), dma((X,)), dma((X,)), dma((Y,)), dma((Y,)),
        dma((8, 2)), dma((8, 2)),
    ]
    shapes = [
        (row_total, later), (1, 1), (RY, C), (10, C), (1, C), (1, C), (1, C), (1, C),
    ]
    whole = pl.BlockSpec(memory_space=pltpu.VMEM)
    scalars = pl.BlockSpec(memory_space=pltpu.SMEM)
    sums = pl.pallas_call(
        functools.partial(kernel, sizes),
        out_shape=[jax.ShapeDtypeStruct(s, F32) for s in (shapes[0], shapes[2], (2, TILES // 2, 8, 128))],
        in_specs=[whole, whole, scalars, scalars] + [whole] * 6,
        out_specs=[whole] * 3,
        scratch_shapes=scratch,
        compiler_params=pltpu.CompilerParams(
            collective_id=0, has_side_effects=True, vmem_limit_bytes=56 * 2**20
        ),
    )(
        waveform, targets, owner_of, lengths, first_weight, first_gain[None], first_shift[None],
        second_weight, second_gain[None], second_shift[None],
    )
    out = pl.pallas_call(
        write_kernel,
        out_shape=[jax.ShapeDtypeStruct(s, F32) for s in shapes],
        in_specs=[whole] * 3,
        out_specs=[whole] * len(shapes),
    )(*sums)
    lv, loss, gw2, gw1, gg1, gs1, gg2, gs2 = out
    return lv, loss[0, 0], gw2, gw1, gg1[0], gs1[0], gg2[0], gs2[0]


def solution(mesh):
    dp, fsdp = mesh.shape["dp"], mesh.shape["fsdp"]
    x = 4 if dp >= 64 else 2
    z = dp // (2 * x)
    torus = Mesh(mesh.devices.reshape(z, x, 2, fsdp), ("dp_0", "dp_1", "dp_2", "fsdp"))
    return jax.shard_map(
        functools.partial(per_device, (z, x, fsdp)),
        mesh=torus,
        in_specs=(
            P(DP_FSDP, None), P(DP_FSDP), P(DP_FSDP), P(DP_FSDP, None), P(), P(), P(),
            P("fsdp", None), P(), P(),
        ),
        out_specs=(P(DP_FSDP, None), P(), P("fsdp", None), P(), P(), P(), P(), P()),
        check_vma=False,
    )
```

```python
import functools

import jax
import jax.numpy as jnp
from jax import lax
from jax.experimental import pallas as pl
from jax.experimental.pallas import tpu as pltpu
from jax.sharding import Mesh
from jax.sharding import PartitionSpec as P

DP = ("dp_0", "dp_1", "dp_2")
DP_FSDP = ("dp_0", "dp_1", "dp_2", "fsdp")
AXES = {"z": "dp_0", "x": "dp_1", "c": "dp_2", "y": "fsdp"}
EPS = 1e-05
C = 512
F32 = jnp.float32
BF16 = jnp.bfloat16
MESH = pl.DeviceIdType.MESH
TN = (((0,), (0,)), ((), ()))
NT = (((1,), (1,)), ((), ()))
TILES = 16
CHUNK = 32
LN2 = 0.6931471805599453
LOG2E = 1.4426950408889634


class Exchange:
    def __init__(self, axis, size, me, src, dst, sems):
        self.axis, self.size, self.me = axis, size, me
        self.src, self.dst = src, dst
        self.send_sems, self.recv_sems = sems

    def _copy(self, r, slot, peer):
        return pltpu.make_async_remote_copy(
            src_ref=self.src(peer),
            dst_ref=self.dst(slot),
            send_sem=self.send_sems.at[r],
            recv_sem=self.recv_sems.at[r],
            device_id={AXES[self.axis]: peer},
            device_id_type=MESH,
        )

    def start(self):
        for r in sorted(range(1, self.size), key=lambda r: -min(r, self.size - r)):
            self._copy(r, self.me, lax.rem(self.me + r, self.size)).start()

    def sender(self, r):
        return lax.rem(self.me + self.size - r, self.size)

    def wait_recv(self, r):
        s = self.sender(r)
        self._copy(r, s, s).wait_recv()

    def wait_all_recv(self):
        for r in range(1, self.size):
            self.wait_recv(r)

    def wait_sends(self):
        for r in range(1, self.size):
            self._copy(r, self.me, lax.rem(self.me + r, self.size)).wait_send()


def dot(a, b, dims=(((1,), (0,)), ((), ()))):
    return lax.dot_general(a, b, dims, preferred_element_type=F32)


def split2(v):
    hi = v.astype(BF16)
    return hi, (v - hi.astype(F32)).astype(BF16)


def split3(v):
    hi, mid = split2(v)
    return hi, mid, (v - hi.astype(F32) - mid.astype(F32)).astype(BF16)


def gelu_parts(u):
    a = jnp.abs(u)
    t = 1.0 / (1.0 + 0.23164190 * a)
    e = jnp.exp(u * u * -0.5)
    poly = 0.5 * 1.061405429
    poly = poly * t - 0.5 * 1.453152027
    poly = poly * t + 0.5 * 1.421413741
    poly = poly * t - 0.5 * 0.284496736
    poly = poly * t + 0.5 * 0.254829592
    tail = poly * t * e
    cdf = jnp.where(u >= 0.0, 1.0 - tail, tail)
    return u * cdf, cdf + u * (e * 0.3989422804014327)


def power_of(top):
    return jnp.ceil(jnp.log(jnp.maximum(top, 1e-30)) * LOG2E + 0.01) - 15.0


def fold8(v):
    return v.reshape(v.shape[0] // 8, 8, v.shape[1]).sum(axis=0)


def kernel(sizes, *refs):
    Z, X, Y = sizes
    (wave_ref, tgt_ref, own_ref, len_ref, fw_ref, g1_ref, s1_ref, w_ref, g2_ref, s2_ref,
     lv_ref, gw2_ref, small_ref,
     W, TG, LG, blk, wpad, wconv, xcol, xh, dg, rs, act, act_peer, v, tsel, vmask, gf, G, g_peer,
     DA, DB, QA, QB, RA, RB, A1, B1, RA2, RB2, XR, dact, gph, gpm, S, S_peer, SY, S1, SZ, SX, SA, pick, FQ,
     w_sy, w_ry, w_sd, w_rd, w_sx, w_rx, w_sc, w_rc, tx_s, tx_r, tz_s, tz_r, lx_s, lx_r, lz_s, lz_r,
     a_s, a_r, b_s, b_r, a2_s, a2_r, b2_s, b2_r, x_s, x_r, z_s, z_r,
     sy_s, sy_r, sz_s, sz_r, sx_s, sx_r, sa_s, sa_r, c_s, c_r) = refs
    z, x, c, y = (lax.axis_index(AXES[k]) for k in "zxcy")
    other = 1 - c
    RY = W.shape[1]
    routed = RY // 2
    halves = X // 2
    RX = routed // halves
    RZ = RY // Z
    rows = 8 * 40
    per_y = TILES // 2 // Y
    dp = Z * X * 2
    readers = dp * 8
    me_dp = (z * X + x) * 2 + c

    barrier = pltpu.get_barrier_semaphore()
    for axis, size, me in (("c", 2, c), ("x", X, x), ("y", Y, y), ("z", Z, z)):
        for r in range(1, size):
            pl.semaphore_signal(
                barrier, inc=1, device_id={AXES[axis]: lax.rem(me + r, size)}, device_id_type=MESH
            )

    def core_copy(k, src, dst):
        return Exchange("c", 2, c, lambda p: src, dst, (c_s.at[k], c_r.at[k]))

    half = pl.ds(pl.multiple_of(c * 256, 256), 256)

    W[y] = w_ref[...]
    r8 = lax.broadcasted_iota(jnp.int32, (8, 128), 0)
    l8 = lax.broadcasted_iota(jnp.int32, (8, 128), 1)
    numbers = jnp.zeros((8, 128), jnp.int32)
    for k in range(8):
        valid = ((len_ref[k] - 10) // 5 - 2) // 2 + 1
        numbers = jnp.where(r8 == k, jnp.where(l8 == 39, own_ref[k], valid), numbers)
    blk[...] = numbers.astype(F32)
    blk[:, : tgt_ref.shape[1]] = tgt_ref[...]
    TG[z, x, c] = blk[...]

    def part_rows(k):
        return pl.ds(pl.multiple_of(k % halves * RX, 16), RX)

    def part_lanes(k):
        return pl.ds(pl.multiple_of(c * 256 + k // halves * 128, 128), 128)

    pl.semaphore_wait(barrier, 1 + (X - 1) + (Y - 1) + (Z - 1))

    wy = Exchange(
        "y", Y, y, lambda p: W.at[y, part_rows(x), part_lanes(x)],
        lambda s: W.at[s, part_rows(x), part_lanes(x)], (w_sy, w_ry),
    )
    wy.start()
    rest = pl.ds(routed, RY - routed)
    wd = Exchange("y", Y, y, lambda p: W.at[y, rest, half], lambda s: W.at[s, rest, half], (w_sd, w_rd))

    def wx(k, slot):
        return Exchange(
            "x", X, x, lambda p: W.at[slot, part_rows(x), part_lanes(x)],
            lambda s: W.at[slot, part_rows(s), part_lanes(s)], (w_sx.at[k], w_rx.at[k]),
        )

    def half_of(k):
        return pl.ds(pl.multiple_of(k * 256, 256), 256)

    def wc(k, slot):
        return Exchange(
            "c", 2, c, lambda p: W.at[slot, :, half], lambda s: W.at[slot, :, half_of(s)],
            (w_sc.at[k], w_rc.at[k]),
        )

    wxs = [wx(r, wy.sender(r)) for r in range(1, Y)]
    wcs = [wc(r, wy.sender(r)) for r in range(1, Y)]
    tz = Exchange("z", Z, z, lambda p: TG.at[z, x, c], lambda s: TG.at[s, x, c], (tz_s, tz_r))
    tz.start()
    tx = Exchange("x", X, x, lambda p: TG.at[:, x, c], lambda s: TG.at[:, s, c], (tx_s, tx_r))
    tc = core_copy(0, TG.at[:, :, c], lambda s: TG.at[:, :, s])

    wpad[...] = jnp.zeros_like(wpad)
    wpad[:, : wave_ref.shape[1]] = wave_ref[...]
    samples = lax.broadcasted_iota(jnp.int32, (512, 128), 0).astype(F32)
    lanes = lax.broadcasted_iota(jnp.int32, (512, 128), 1).astype(F32)
    tap = samples - 5.0 * jnp.floor((samples + 0.5) * 0.2)
    place_hi = jnp.where((lanes == tap) | (lanes == tap + 16.0), 1.0, 0.0).astype(BF16)
    place_mid = jnp.where(lanes == tap + 8.0, 1.0, 0.0).astype(BF16)
    frame = lax.broadcasted_iota(jnp.int32, (40, 512), 0)
    offset = lax.broadcasted_iota(jnp.int32, (40, 512), 1) - 10 * frame
    in_even = (offset >= 0) & (offset < 5)
    in_odd = (offset >= 5) & (offset < 10)
    even, odd = [], []
    for k in range(8):
        row = jnp.broadcast_to(wpad[k : k + 1, :], (40, 512))
        even.append(jnp.where(in_even, row, 0.0))
        odd.append(jnp.where(in_odd, row, 0.0))
    blocks = []
    for parts in (even, odd):
        hi, mid = split2(jnp.concatenate(parts, axis=0))
        blocks.append(dot(hi, place_hi) + dot(mid, place_mid))
    even_block, odd_block = blocks
    xcol[:rows] = (even_block + pltpu.roll(odd_block, 32, 1)).astype(BF16)
    xcol[rows:] = (odd_block + pltpu.roll(pltpu.roll(even_block, rows - 1, 0), 32, 1)).astype(BF16)
    wconv[...] = jnp.zeros_like(wconv)
    fw = fw_ref[...]
    fw_hi = fw.astype(BF16).astype(F32)
    fw_mid = (fw - fw_hi).astype(BF16).astype(F32)
    for base, taps in ((0, slice(0, 5)), (32, slice(5, 10))):
        wconv[base : base + 5] = fw_hi[taps]
        wconv[base + 8 : base + 13] = fw_hi[taps]
        wconv[base + 16 : base + 21] = fw_mid[taps]
    xh[...] = dot(xcol[...], wconv[...].astype(BF16))

    wd.start()
    g1, s1 = g1_ref[...], s1_ref[...]

    def forward_chunk(i, carry):
        at = pl.ds(pl.multiple_of(i * CHUNK, CHUNK), CHUNK)
        pre = xh[at, :]
        centered = pre - jnp.mean(pre, axis=1, keepdims=True)
        inv = lax.rsqrt(jnp.mean(centered * centered, axis=1, keepdims=True) + EPS)
        normed = centered * inv
        value, slope = gelu_parts(normed * g1 + s1)
        xh[at, :] = normed
        dg[at, :] = slope
        rs[at, :] = jnp.broadcast_to(inv, (CHUNK, 128))
        act[at, :] = value.astype(BF16)
        return carry

    chunks = 2 * rows // CHUNK
    near_first = sorted(range(1, Y), key=lambda r: min(r, Y - r))
    steps = 4
    for k in range(steps):
        for r in near_first[k * 2 : (k + 1) * 2 if k < 2 else Y] if k < 3 else ():
            wy.wait_recv(r)
            wxs[r - 1].start()
        if k == 1:
            tz.wait_all_recv()
            tx.start()
        if k == 3:
            tx.wait_all_recv()
            tc.start()
        lax.fori_loop(chunks * k // steps, chunks * (k + 1) // steps, forward_chunk, 0, unroll=True)
    act_send = core_copy(1, act, lambda s: act_peer)
    act_send.start()
    for r in near_first:
        wxs[r - 1].wait_all_recv()
        wd.wait_recv(r)
        wcs[r - 1].start()

    tc.wait_all_recv()
    table = TG[...].reshape(readers, 128)
    owner_col = table[:, 39:40]
    mine = blk[...]
    owner_row = jnp.sum(jnp.where(r8 == l8, mine[:, 39:40], 0.0), axis=0, keepdims=True)
    rr = lax.broadcasted_iota(jnp.int32, (readers, 128), 0)
    ll = lax.broadcasted_iota(jnp.int32, (readers, 128), 1)
    before = jnp.sum(
        jnp.where((owner_col == owner_row) & (rr < me_dp * 8), 1.0, 0.0), axis=0, keepdims=True
    )
    wanted = owner_row * 8.0 + before
    one_hot = jnp.where((rr.astype(F32) == wanted) & (ll < 8), 1.0, 0.0).astype(BF16)
    found = sum(dot(one_hot, part, TN) for part in split3(table))
    tsel[...] = found[:8]
    vmask[...] = jnp.where(l8.astype(F32) < mine[:, 40:41], 1.0, 0.0)
    flags = jnp.where(owner_col == me_dp.astype(F32), 1.0, 0.0)
    flags = jnp.broadcast_to(flags, (readers, 128))
    lower = lax.broadcasted_iota(jnp.int32, (readers, readers), 0) > lax.broadcasted_iota(
        jnp.int32, (readers, readers), 1
    )
    place = dot(jnp.where(lower, 1.0, 0.0).astype(BF16), flags.astype(BF16))
    pick[...] = jnp.where((flags > 0.5) & (place == ll.astype(F32)), 1.0, 0.0).astype(BF16)

    for e in wcs:
        e.wait_all_recv()

    def tap_weight(q):
        return W[...].reshape(3 * C, C)[q * C : (q + 1) * C]

    act_even, act_odd = act[:rows], act[rows:]
    later = dot(act_even, tap_weight(2))
    v[...] = dot(act_even, tap_weight(0)) + dot(act_odd, tap_weight(1)) + pltpu.roll(later, rows - 1, 0)

    g2, s2 = g2_ref[...], s2_ref[...]
    eye = lax.broadcasted_iota(jnp.int32, (40, 128), 0) == lax.broadcasted_iota(jnp.int32, (40, 128), 1)

    def head_row(k, carry):
        gain_sum, shift_sum, misfit_sum, count = carry
        at = pl.ds(pl.multiple_of(k * 40, 8), 40)
        target = jnp.sum(jnp.where(eye, tsel[pl.ds(k, 1), :], 0.0), axis=1, keepdims=True)
        mask = jnp.sum(jnp.where(eye, vmask[pl.ds(k, 1), :], 0.0), axis=1, keepdims=True)
        pre = v[at, :]
        centered = pre - jnp.mean(pre, axis=1, keepdims=True)
        inv = lax.rsqrt(jnp.mean(centered * centered, axis=1, keepdims=True) + EPS)
        normed = centered * inv
        value, slope = gelu_parts(normed * g2 + s2)
        centered = value - jnp.mean(value, axis=1, keepdims=True)
        spread = jnp.mean(centered * centered, axis=1, keepdims=True) + EPS
        raw = jnp.log(spread)
        misfit = raw - target
        LG[z, x, c, pl.ds(k, 1), :] = jnp.sum(jnp.where(eye, raw * mask, 0.0), axis=0, keepdims=True)
        du = centered * (mask * misfit * (4.0 / C) / spread) * slope
        dx = du * g2
        m1 = jnp.mean(dx, axis=1, keepdims=True)
        m2 = jnp.mean(dx * normed, axis=1, keepdims=True)
        gf[at, :] = inv * (dx - m1 - normed * m2)
        return (
            gain_sum + fold8(du * normed),
            shift_sum + fold8(du),
            misfit_sum + mask * misfit * misfit,
            count + mask,
        )

    zero = jnp.zeros((8, C), F32)
    column = jnp.zeros((40, 1), F32)
    gain_sum2, shift_sum2, misfit_sum, count = lax.fori_loop(0, 8, head_row, (zero, zero, column, column), unroll=8)
    lz = Exchange("z", Z, z, lambda p: LG.at[z, x, c], lambda s: LG.at[s, x, c], (lz_s, lz_r))
    lz.start()
    grad = gf[...]
    grad_late = pltpu.roll(grad, 1, 0)
    for h in range(2):
        G[h, 0] = grad[:, 256 * h : 256 * (h + 1)].astype(BF16)
        G[h, 1] = grad_late[:, 256 * h : 256 * (h + 1)].astype(BF16)
    g_send = core_copy(2, G.at[other], lambda s: g_peer)
    g_send.start()

    def column_grads(acts, grads):
        e, o = acts[:rows], acts[rows:]
        return dot(e, grads[0], TN), dot(o, grads[0], TN), dot(e, grads[1], TN)

    own = column_grads(act, G.at[c])
    lx = Exchange("x", X, x, lambda p: LG.at[:, x, c], lambda s: LG.at[:, s, c], (lx_s, lx_r))
    lc = core_copy(3, LG.at[:, :, c], lambda s: LG.at[:, :, s])
    act_send.wait_all_recv()
    g_send.wait_all_recv()
    peers = column_grads(act_peer, g_peer)
    total = jnp.concatenate([a + b for a, b in zip(own, peers)], axis=0)
    DA[...] = total[:, :128].reshape(Y, RY, 128)
    DB[...] = total[:, 128:].reshape(Y, Z, RZ, 128).transpose(1, 0, 2, 3).reshape(Z, Y * RZ, 128)
    def encode(full, coded):
        values = full[...]
        n, height, width = values.shape
        top = jnp.max(jnp.abs(values).reshape(n * height, width), axis=0, keepdims=True)
        power = power_of(top)
        ratio = jnp.exp(power * -LN2)
        coded[:, :height] = jnp.round(values * ratio[None]).astype(jnp.int32).astype(jnp.int16)
        code = jnp.broadcast_to(power, (16, width)).astype(jnp.int32).astype(jnp.int16)
        for k in range(n):
            coded[k, height:] = code

    def decoded(slot):
        height = slot.shape[0] - 16
        power = slot[height:, :].astype(jnp.int32).astype(F32)[0:1]
        return slot[:height, :].astype(jnp.int32).astype(F32) * jnp.exp(power * LN2)

    ya = Exchange("y", Y, y, lambda p: QA.at[p], lambda s: RA.at[s], (a_s, a_r))
    zb = Exchange("z", Z, z, lambda p: QB.at[p], lambda s: RB.at[s], (b_s, b_r))
    encode(DA, QA)
    ya.start()
    encode(DB, QB)
    zb.start()
    lz.wait_all_recv()
    lx.start()

    def whole_grad(k):
        return jnp.concatenate([G[0, k], G[1, k]], axis=1)

    now, late = whole_grad(0), whole_grad(1)
    dact[:rows] = dot(now, tap_weight(0), NT) + dot(late, tap_weight(2), NT)
    dact[rows:] = dot(now, tap_weight(1), NT)

    def backward_chunk(i, carry):
        gain_sum, shift_sum = carry
        at = pl.ds(pl.multiple_of(i * CHUNK, CHUNK), CHUNK)
        normed = xh[at, :]
        du = dact[at, :] * dg[at, :]
        dx = du * g1
        m1 = jnp.mean(dx, axis=1, keepdims=True)
        m2 = jnp.mean(dx * normed, axis=1, keepdims=True)
        dpre = rs[at, :1] * (dx - m1 - normed * m2)
        hi, mid = split2(dpre)
        gph[at, :] = hi
        gpm[at, :] = mid
        return gain_sum + fold8(du * normed), shift_sum + fold8(du)

    gain_sum1, shift_sum1 = lax.fori_loop(0, chunks, backward_chunk, (zero, zero), unroll=2)
    taps = dot(xcol[...], gph[...], TN) + dot(xcol[...], gpm[...], TN)
    ri = lax.broadcasted_iota(jnp.int32, (8, C), 0)
    li = lax.broadcasted_iota(jnp.int32, (8, C), 1)

    def line(vector, k):
        return jnp.where(ri == k, jnp.sum(vector, axis=0, keepdims=True), 0.0)

    loss_line = jnp.where(
        li == 0,
        jnp.sum(misfit_sum, axis=0, keepdims=True),
        jnp.where(li == 1, jnp.sum(count, axis=0, keepdims=True), 0.0),
    )
    groups = [
        taps[0:8] + taps[8:16],
        taps[32:40] + taps[40:48],
        line(gain_sum1, 0) + line(shift_sum1, 1) + line(gain_sum2, 2) + line(shift_sum2, 3)
        + jnp.where(ri == 4, loss_line, 0.0),
        zero,
    ]
    for i, group in enumerate(groups):
        for j in range(4):
            S[i // 2, 4 * (i % 2) + j] = group[:, 128 * j : 128 * (j + 1)]
    sc = core_copy(4, S.at[other], lambda s: S_peer)
    sc.start()
    lx.wait_all_recv()
    lc.start()
    sc.wait_all_recv()
    S1[...] = (S[c] + S_peer[...]).reshape(Y, per_y, 8, 128)
    sy = Exchange("y", Y, y, lambda p: S1.at[p], lambda s: SY.at[s], (sy_s, sy_r))
    sy.start()

    total = DA[y]
    for r in range(1, Y):
        ya.wait_recv(r)
        total = total + decoded(RA.at[ya.sender(r)])
    A1[...] = total.reshape(Z, RZ, 128)
    za = Exchange("z", Z, z, lambda p: A1.at[p], lambda s: RA2.at[s], (a2_s, a2_r))
    za.start()
    total = DB[z]
    for r in range(1, Z):
        zb.wait_recv(r)
        total = total + decoded(RB.at[zb.sender(r)])
    B1[...] = total.reshape(Y, RZ, 128)
    yb = Exchange("y", Y, y, lambda p: B1.at[p], lambda s: RB2.at[s], (b2_s, b2_r))
    yb.start()
    sy.wait_all_recv()
    SY[y] = S1[y]
    total = SY[0]
    for k in range(1, Y):
        total = total + SY[k]
    SZ[z] = total
    sz = Exchange("z", Z, z, lambda p: SZ.at[z], lambda s: SZ.at[s], (sz_s, sz_r))
    sz.start()

    first = A1[z]
    for r in range(1, Z):
        za.wait_recv(r)
        first = first + RA2[za.sender(r)]
    second = B1[y]
    for r in range(1, Y):
        yb.wait_recv(r)
        second = second + RB2[yb.sender(r)]
    XR[x] = jnp.concatenate([first, second], axis=1)
    xs = Exchange("x", X, x, lambda p: XR.at[x], lambda s: XR.at[s], (x_s, x_r))
    xs.start()
    sz.wait_all_recv()
    total = SZ[0]
    for k in range(1, Z):
        total = total + SZ[k]
    SX[x] = total
    sx = Exchange("x", X, x, lambda p: SX.at[x], lambda s: SX.at[s], (sx_s, sx_r))
    sx.start()

    xs.wait_all_recv()
    total = XR[0]
    for k in range(1, X):
        total = total + XR[k]
    power = power_of(jnp.max(jnp.abs(total), axis=0, keepdims=True))
    spare = FQ.shape[2] - RZ
    codes = jnp.concatenate(
        [jnp.round(total * jnp.exp(power * -LN2)), jnp.broadcast_to(power, (spare, 256))], axis=0
    )
    FQ[c, z] = codes.astype(jnp.int32).astype(jnp.int16)
    zg = Exchange("z", Z, z, lambda p: FQ.at[c, z], lambda s: FQ.at[c, s], (z_s, z_r))
    zg.start()
    sx.wait_all_recv()
    total = SX[0]
    for k in range(1, X):
        total = total + SX[k]
    SA[y] = total
    sa = Exchange("y", Y, y, lambda p: SA.at[y], lambda s: SA.at[s], (sa_s, sa_r))
    sa.start()

    lc.wait_all_recv()
    logs = LG[...].reshape(readers, 128)
    picked = sum(dot(pick[...], part, TN) for part in split3(logs))
    lv_ref[...] = picked[:8, : lv_ref.shape[1]]

    zg.wait_all_recv()
    fin = core_copy(5, FQ.at[c], lambda s: FQ.at[s])
    fin.start()

    sa.wait_all_recv()
    small_ref[c] = SA[...].reshape(TILES // 2, 8, 128)
    sf = core_copy(6, small_ref.at[c], lambda s: small_ref.at[s])
    sf.start()
    sf.wait_all_recv()
    fin.wait_all_recv()
    for h in range(2):
        for k in range(Z):
            piece = FQ[h, k].astype(jnp.int32).astype(F32)
            gw2_ref[k * RZ : (k + 1) * RZ, 256 * h : 256 * (h + 1)] = piece[:RZ] * jnp.exp(
                piece[RZ : RZ + 1] * LN2
            )

    waiting = [wy, wd, tc, tx, tz, act_send, g_send, lc, lx, lz, ya, zb, za, yb, xs, zg, sc, sy, sz, sx, sa, sf, fin]
    for e in waiting + wxs + wcs:
        e.wait_sends()


def write_kernel(lv_in, gw2_in, small, lv_ref, loss_ref, gw2_ref, gw1_ref, gg1_ref, gs1_ref, gg2_ref, gs2_ref):
    def wide(i):
        return jnp.concatenate([small[i // 2, 4 * (i % 2) + j] for j in range(4)], axis=1)

    lv_ref[...] = lv_in[...]
    gw2_ref[...] = gw2_in[...]
    gw1_ref[0:5] = wide(0)[0:5]
    gw1_ref[5:10] = wide(1)[0:5]
    norms = wide(2)
    gg1_ref[...] = norms[0:1]
    gs1_ref[...] = norms[1:2]
    gg2_ref[...] = norms[2:3]
    gs2_ref[...] = norms[3:4]
    loss_ref[...] = norms[4:5, 0:1] / norms[4:5, 1:2]


def per_device(sizes, waveform, lengths, owner_of, targets, first_weight, first_gain, first_shift,
               second_weight, second_gain, second_shift):
    Z, X, Y = sizes
    row_total, later = targets.shape
    RY = second_weight.shape[0]
    RZ = RY // Z
    rows = 320
    dma = pltpu.SemaphoreType.DMA
    vm = pltpu.VMEM
    per_y = TILES // 2 // Y
    scratch = [
        vm((Y, RY, C), BF16), vm((Z, X, 2, 8, 128), F32), vm((Z, X, 2, 8, 128), F32), vm((8, 128), F32),
        vm((8, 512), F32), vm((128, C), F32), vm((2 * rows, 128), BF16),
        vm((2 * rows, C), F32), vm((2 * rows, C), F32), vm((2 * rows, 128), F32),
        vm((2 * rows, C), BF16), vm((2 * rows, C), BF16), vm((rows, C), F32),
        vm((8, 128), F32), vm((8, 128), F32), vm((rows, C), F32),
        vm((2, 2, rows, 256), BF16), vm((2, rows, 256), BF16),
        vm((Y, RY, 128), F32), vm((Z, Y * RZ, 128), F32),
        vm((Y, RY + 16, 128), jnp.int16), vm((Z, Y * RZ + 16, 128), jnp.int16),
        vm((Y, RY + 16, 128), jnp.int16), vm((Z, Y * RZ + 16, 128), jnp.int16),
        vm((Z, RZ, 128), F32), vm((Y, RZ, 128), F32), vm((Z, RZ, 128), F32), vm((Y, RZ, 128), F32),
        vm((X, RZ, 256), F32), vm((2 * rows, C), F32), vm((2 * rows, C), BF16), vm((2 * rows, C), BF16),
        vm((2, TILES // 2, 8, 128), F32), vm((TILES // 2, 8, 128), F32), vm((Y, per_y, 8, 128), F32),
        vm((Y, per_y, 8, 128), F32), vm((Z, per_y, 8, 128), F32), vm((X, per_y, 8, 128), F32),
        vm((Y, per_y, 8, 128), F32), vm((Z * X * 2 * 8, 128), BF16),
        vm((2, Z, RZ + (8 if RZ % 16 else 16), 256), jnp.int16),
        dma((Y,)), dma((Y,)), dma((Y,)), dma((Y,)), dma((Y, X)), dma((Y, X)), dma((Y, 2)), dma((Y, 2)),
        dma((X,)), dma((X,)), dma((Z,)), dma((Z,)), dma((X,)), dma((X,)), dma((Z,)), dma((Z,)),
        dma((Y,)), dma((Y,)), dma((Z,)), dma((Z,)), dma((Z,)), dma((Z,)), dma((Y,)), dma((Y,)),
        dma((X,)), dma((X,)), dma((Z,)), dma((Z,)),
        dma((Y,)), dma((Y,)), dma((Z,)), dma((Z,)), dma((X,)), dma((X,)), dma((Y,)), dma((Y,)),
        dma((8, 2)), dma((8, 2)),
    ]
    shapes = [
        (row_total, later), (1, 1), (RY, C), (10, C), (1, C), (1, C), (1, C), (1, C),
    ]
    whole = pl.BlockSpec(memory_space=pltpu.VMEM)
    scalars = pl.BlockSpec(memory_space=pltpu.SMEM)
    sums = pl.pallas_call(
        functools.partial(kernel, sizes),
        out_shape=[jax.ShapeDtypeStruct(s, F32) for s in (shapes[0], shapes[2], (2, TILES // 2, 8, 128))],
        in_specs=[whole, whole, scalars, scalars] + [whole] * 6,
        out_specs=[whole] * 3,
        scratch_shapes=scratch,
        compiler_params=pltpu.CompilerParams(
            collective_id=0, has_side_effects=True, vmem_limit_bytes=56 * 2**20
        ),
    )(
        waveform, targets, owner_of, lengths, first_weight, first_gain[None], first_shift[None],
        second_weight, second_gain[None], second_shift[None],
    )
    out = pl.pallas_call(
        write_kernel,
        out_shape=[jax.ShapeDtypeStruct(s, F32) for s in shapes],
        in_specs=[whole] * 3,
        out_specs=[whole] * len(shapes),
    )(*sums)
    lv, loss, gw2, gw1, gg1, gs1, gg2, gs2 = out
    return lv, loss[0, 0], gw2, gw1, gg1[0], gs1[0], gg2[0], gs2[0]


def solution(mesh):
    dp, fsdp = mesh.shape["dp"], mesh.shape["fsdp"]
    x = 4 if dp >= 64 else 2
    z = dp // (2 * x)
    torus = Mesh(mesh.devices.reshape(z, x, 2, fsdp), ("dp_0", "dp_1", "dp_2", "fsdp"))
    return jax.shard_map(
        functools.partial(per_device, (z, x, fsdp)),
        mesh=torus,
        in_specs=(
            P(DP_FSDP, None), P(DP_FSDP), P(DP_FSDP), P(DP_FSDP, None), P(), P(), P(),
            P("fsdp", None), P(), P(),
        ),
        out_specs=(P(DP_FSDP, None), P(), P("fsdp", None), P(), P(), P(), P(), P()),
        check_vma=False,
    )
```

```python
import functools

import jax
import jax.numpy as jnp
from jax import lax
from jax.experimental import pallas as pl
from jax.experimental.pallas import tpu as pltpu
from jax.sharding import Mesh
from jax.sharding import PartitionSpec as P

DP = ("dp_0", "dp_1", "dp_2")
DP_FSDP = ("dp_0", "dp_1", "dp_2", "fsdp")
AXES = {"z": "dp_0", "x": "dp_1", "c": "dp_2", "y": "fsdp"}
EPS = 1e-05
C = 512
F32 = jnp.float32
BF16 = jnp.bfloat16
MESH = pl.DeviceIdType.MESH
TN = (((0,), (0,)), ((), ()))
NT = (((1,), (1,)), ((), ()))
TILES = 16
CHUNK = 32
LN2 = 0.6931471805599453
LOG2E = 1.4426950408889634


class Exchange:
    def __init__(self, axis, size, me, src, dst, sems):
        self.axis, self.size, self.me = axis, size, me
        self.src, self.dst = src, dst
        self.send_sems, self.recv_sems = sems

    def _copy(self, r, slot, peer):
        return pltpu.make_async_remote_copy(
            src_ref=self.src(peer),
            dst_ref=self.dst(slot),
            send_sem=self.send_sems.at[r],
            recv_sem=self.recv_sems.at[r],
            device_id={AXES[self.axis]: peer},
            device_id_type=MESH,
        )

    def start(self):
        for r in sorted(range(1, self.size), key=lambda r: -min(r, self.size - r)):
            self._copy(r, self.me, lax.rem(self.me + r, self.size)).start()

    def sender(self, r):
        return lax.rem(self.me + self.size - r, self.size)

    def wait_recv(self, r):
        s = self.sender(r)
        self._copy(r, s, s).wait_recv()

    def wait_all_recv(self):
        for r in range(1, self.size):
            self.wait_recv(r)

    def wait_sends(self):
        for r in range(1, self.size):
            self._copy(r, self.me, lax.rem(self.me + r, self.size)).wait_send()


def dot(a, b, dims=(((1,), (0,)), ((), ()))):
    return lax.dot_general(a, b, dims, preferred_element_type=F32)


def split2(v):
    hi = v.astype(BF16)
    return hi, (v - hi.astype(F32)).astype(BF16)


def split3(v):
    hi, mid = split2(v)
    return hi, mid, (v - hi.astype(F32) - mid.astype(F32)).astype(BF16)


def gelu_parts(u):
    a = jnp.abs(u)
    t = 1.0 / (1.0 + 0.23164190 * a)
    e = jnp.exp(u * u * -0.5)
    poly = 0.5 * 1.061405429
    poly = poly * t - 0.5 * 1.453152027
    poly = poly * t + 0.5 * 1.421413741
    poly = poly * t - 0.5 * 0.284496736
    poly = poly * t + 0.5 * 0.254829592
    tail = poly * t * e
    cdf = jnp.where(u >= 0.0, 1.0 - tail, tail)
    return u * cdf, cdf + u * (e * 0.3989422804014327)


def power_of(top):
    return jnp.ceil(jnp.log(jnp.maximum(top, 1e-30)) * LOG2E + 0.01) - 15.0


def fold8(v):
    return v.reshape(v.shape[0] // 8, 8, v.shape[1]).sum(axis=0)


def kernel(sizes, *refs):
    Z, X, Y = sizes
    (wave_in, tgt_in, own_in, len_in, fw_in, g1_in, s1_in, w_in, g2_in, s2_in,
     lv_ref, gw2_ref, small_ref,
     wave_ref, tgt_ref, own_ref, len_ref, fw_ref, g1_ref, s1_ref, g2_ref, s2_ref, in_s,
     W, TG, LG, blk, wpad, wconv, xcol, xh, dg, rs, act, act_peer, v, tsel, vmask, gf, G, g_peer,
     DA, DB, QA, QB, RA, RB, A1, B1, RA2, RB2, XR, dact, gph, gpm, S, S_peer, SY, S1, SZ, SX, SA, pick, FQ,
     w_sy, w_ry, w_sd, w_rd, w_sx, w_rx, w_sc, w_rc, tx_s, tx_r, tz_s, tz_r, lx_s, lx_r, lz_s, lz_r,
     a_s, a_r, b_s, b_r, a2_s, a2_r, b2_s, b2_r, x_s, x_r, z_s, z_r,
     sy_s, sy_r, sz_s, sz_r, sx_s, sx_r, sa_s, sa_r, c_s, c_r) = refs
    z, x, c, y = (lax.axis_index(AXES[k]) for k in "zxcy")
    other = 1 - c
    RY = W.shape[1]
    routed = RY // 2
    halves = X // 2
    RX = routed // halves
    RZ = RY // Z
    rows = 8 * 40
    per_y = TILES // 2 // Y
    dp = Z * X * 2
    readers = dp * 8
    me_dp = (z * X + x) * 2 + c

    barrier = pltpu.get_barrier_semaphore()
    for axis, size, me in (("c", 2, c), ("x", X, x), ("y", Y, y), ("z", Z, z)):
        for r in range(1, size):
            pl.semaphore_signal(
                barrier, inc=1, device_id={AXES[axis]: lax.rem(me + r, size)}, device_id_type=MESH
            )

    def core_copy(k, src, dst):
        return Exchange("c", 2, c, lambda p: src, dst, (c_s.at[k], c_r.at[k]))

    half = pl.ds(pl.multiple_of(c * 256, 256), 256)

    loads = [
        pltpu.make_async_copy(source, target, in_s.at[k])
        for k, (source, target) in enumerate(
            (
                (w_in, W.at[y]), (own_in, own_ref), (len_in, len_ref), (tgt_in, tgt_ref), (wave_in, wave_ref),
                (fw_in, fw_ref), (g1_in, g1_ref), (s1_in, s1_ref), (g2_in, g2_ref), (s2_in, s2_ref),
            )
        )
    ]
    for load in loads:
        load.start()
    for load in loads[:4]:
        load.wait()
    r8 = lax.broadcasted_iota(jnp.int32, (8, 128), 0)
    l8 = lax.broadcasted_iota(jnp.int32, (8, 128), 1)
    numbers = jnp.zeros((8, 128), jnp.int32)
    for k in range(8):
        valid = ((len_ref[k] - 10) // 5 - 2) // 2 + 1
        numbers = jnp.where(r8 == k, jnp.where(l8 == 39, own_ref[k], valid), numbers)
    blk[...] = numbers.astype(F32)
    blk[:, : tgt_ref.shape[1]] = tgt_ref[...]
    TG[z, x, c] = blk[...]

    def part_rows(k):
        return pl.ds(pl.multiple_of(k % halves * RX, 16), RX)

    def part_lanes(k):
        return pl.ds(pl.multiple_of(c * 256 + k // halves * 128, 128), 128)

    pl.semaphore_wait(barrier, 1 + (X - 1) + (Y - 1) + (Z - 1))

    wy = Exchange(
        "y", Y, y, lambda p: W.at[y, part_rows(x), part_lanes(x)],
        lambda s: W.at[s, part_rows(x), part_lanes(x)], (w_sy, w_ry),
    )
    wy.start()
    rest = pl.ds(routed, RY - routed)
    wd = Exchange("y", Y, y, lambda p: W.at[y, rest, half], lambda s: W.at[s, rest, half], (w_sd, w_rd))

    def wx(k, slot):
        return Exchange(
            "x", X, x, lambda p: W.at[slot, part_rows(x), part_lanes(x)],
            lambda s: W.at[slot, part_rows(s), part_lanes(s)], (w_sx.at[k], w_rx.at[k]),
        )

    def half_of(k):
        return pl.ds(pl.multiple_of(k * 256, 256), 256)

    def wc(k, slot):
        return Exchange(
            "c", 2, c, lambda p: W.at[slot, :, half], lambda s: W.at[slot, :, half_of(s)],
            (w_sc.at[k], w_rc.at[k]),
        )

    wxs = [wx(r, wy.sender(r)) for r in range(1, Y)]
    wcs = [wc(r, wy.sender(r)) for r in range(1, Y)]
    tz = Exchange("z", Z, z, lambda p: TG.at[z, x, c], lambda s: TG.at[s, x, c], (tz_s, tz_r))
    tz.start()
    tx = Exchange("x", X, x, lambda p: TG.at[:, x, c], lambda s: TG.at[:, s, c], (tx_s, tx_r))
    tc = core_copy(0, TG.at[:, :, c], lambda s: TG.at[:, :, s])

    for load in loads[4:]:
        load.wait()
    wpad[...] = jnp.zeros_like(wpad)
    wpad[:, : wave_ref.shape[1]] = wave_ref[...]
    samples = lax.broadcasted_iota(jnp.int32, (512, 128), 0).astype(F32)
    lanes = lax.broadcasted_iota(jnp.int32, (512, 128), 1).astype(F32)
    tap = samples - 5.0 * jnp.floor((samples + 0.5) * 0.2)
    place_hi = jnp.where((lanes == tap) | (lanes == tap + 16.0), 1.0, 0.0).astype(BF16)
    place_mid = jnp.where(lanes == tap + 8.0, 1.0, 0.0).astype(BF16)
    frame = lax.broadcasted_iota(jnp.int32, (40, 512), 0)
    offset = lax.broadcasted_iota(jnp.int32, (40, 512), 1) - 10 * frame
    in_even = (offset >= 0) & (offset < 5)
    in_odd = (offset >= 5) & (offset < 10)
    even, odd = [], []
    for k in range(8):
        row = jnp.broadcast_to(wpad[k : k + 1, :], (40, 512))
        even.append(jnp.where(in_even, row, 0.0))
        odd.append(jnp.where(in_odd, row, 0.0))
    blocks = []
    for parts in (even, odd):
        hi, mid = split2(jnp.concatenate(parts, axis=0))
        blocks.append(dot(hi, place_hi) + dot(mid, place_mid))
    even_block, odd_block = blocks
    xcol[:rows] = (even_block + pltpu.roll(odd_block, 32, 1)).astype(BF16)
    xcol[rows:] = (odd_block + pltpu.roll(pltpu.roll(even_block, rows - 1, 0), 32, 1)).astype(BF16)
    wconv[...] = jnp.zeros_like(wconv)
    fw = fw_ref[...]
    fw_hi = fw.astype(BF16).astype(F32)
    fw_mid = (fw - fw_hi).astype(BF16).astype(F32)
    for base, taps in ((0, slice(0, 5)), (32, slice(5, 10))):
        wconv[base : base + 5] = fw_hi[taps]
        wconv[base + 8 : base + 13] = fw_hi[taps]
        wconv[base + 16 : base + 21] = fw_mid[taps]
    xh[...] = dot(xcol[...], wconv[...].astype(BF16))

    wd.start()
    g1, s1 = g1_ref[...], s1_ref[...]

    def forward_chunk(i, carry):
        at = pl.ds(pl.multiple_of(i * CHUNK, CHUNK), CHUNK)
        pre = xh[at, :]
        centered = pre - jnp.mean(pre, axis=1, keepdims=True)
        inv = lax.rsqrt(jnp.mean(centered * centered, axis=1, keepdims=True) + EPS)
        normed = centered * inv
        value, slope = gelu_parts(normed * g1 + s1)
        xh[at, :] = normed
        dg[at, :] = slope
        rs[at, :] = jnp.broadcast_to(inv, (CHUNK, 128))
        act[at, :] = value.astype(BF16)
        return carry

    chunks = 2 * rows // CHUNK
    near_first = sorted(range(1, Y), key=lambda r: min(r, Y - r))
    steps = 4
    for k in range(steps):
        for r in near_first[k * 2 : (k + 1) * 2 if k < 2 else Y] if k < 3 else ():
            wy.wait_recv(r)
            wxs[r - 1].start()
        if k == 1:
            tz.wait_all_recv()
            tx.start()
        if k == 3:
            tx.wait_all_recv()
            tc.start()
        lax.fori_loop(chunks * k // steps, chunks * (k + 1) // steps, forward_chunk, 0, unroll=True)
    act_send = core_copy(1, act, lambda s: act_peer)
    act_send.start()
    for r in near_first:
        wxs[r - 1].wait_all_recv()
        wd.wait_recv(r)
        wcs[r - 1].start()

    tc.wait_all_recv()
    table = TG[...].reshape(readers, 128)
    owner_col = table[:, 39:40]
    mine = blk[...]
    owner_row = jnp.sum(jnp.where(r8 == l8, mine[:, 39:40], 0.0), axis=0, keepdims=True)
    rr = lax.broadcasted_iota(jnp.int32, (readers, 128), 0)
    ll = lax.broadcasted_iota(jnp.int32, (readers, 128), 1)
    before = jnp.sum(
        jnp.where((owner_col == owner_row) & (rr < me_dp * 8), 1.0, 0.0), axis=0, keepdims=True
    )
    wanted = owner_row * 8.0 + before
    one_hot = jnp.where((rr.astype(F32) == wanted) & (ll < 8), 1.0, 0.0).astype(BF16)
    found = sum(dot(one_hot, part, TN) for part in split3(table))
    tsel[...] = found[:8]
    vmask[...] = jnp.where(l8.astype(F32) < mine[:, 40:41], 1.0, 0.0)
    flags = jnp.where(owner_col == me_dp.astype(F32), 1.0, 0.0)
    flags = jnp.broadcast_to(flags, (readers, 128))
    lower = lax.broadcasted_iota(jnp.int32, (readers, readers), 0) > lax.broadcasted_iota(
        jnp.int32, (readers, readers), 1
    )
    place = dot(jnp.where(lower, 1.0, 0.0).astype(BF16), flags.astype(BF16))
    pick[...] = jnp.where((flags > 0.5) & (place == ll.astype(F32)), 1.0, 0.0).astype(BF16)

    for e in wcs:
        e.wait_all_recv()

    def tap_weight(q):
        return W[...].reshape(3 * C, C)[q * C : (q + 1) * C]

    act_even, act_odd = act[:rows], act[rows:]
    later = dot(act_even, tap_weight(2))
    v[...] = dot(act_even, tap_weight(0)) + dot(act_odd, tap_weight(1)) + pltpu.roll(later, rows - 1, 0)

    g2, s2 = g2_ref[...], s2_ref[...]
    eye = lax.broadcasted_iota(jnp.int32, (40, 128), 0) == lax.broadcasted_iota(jnp.int32, (40, 128), 1)

    def head_row(k, carry):
        gain_sum, shift_sum, misfit_sum, count = carry
        at = pl.ds(pl.multiple_of(k * 40, 8), 40)
        target = jnp.sum(jnp.where(eye, tsel[pl.ds(k, 1), :], 0.0), axis=1, keepdims=True)
        mask = jnp.sum(jnp.where(eye, vmask[pl.ds(k, 1), :], 0.0), axis=1, keepdims=True)
        pre = v[at, :]
        centered = pre - jnp.mean(pre, axis=1, keepdims=True)
        inv = lax.rsqrt(jnp.mean(centered * centered, axis=1, keepdims=True) + EPS)
        normed = centered * inv
        value, slope = gelu_parts(normed * g2 + s2)
        centered = value - jnp.mean(value, axis=1, keepdims=True)
        spread = jnp.mean(centered * centered, axis=1, keepdims=True) + EPS
        raw = jnp.log(spread)
        misfit = raw - target
        LG[z, x, c, pl.ds(k, 1), :] = jnp.sum(jnp.where(eye, raw * mask, 0.0), axis=0, keepdims=True)
        du = centered * (mask * misfit * (4.0 / C) / spread) * slope
        dx = du * g2
        m1 = jnp.mean(dx, axis=1, keepdims=True)
        m2 = jnp.mean(dx * normed, axis=1, keepdims=True)
        gf[at, :] = inv * (dx - m1 - normed * m2)
        return (
            gain_sum + fold8(du * normed),
            shift_sum + fold8(du),
            misfit_sum + mask * misfit * misfit,
            count + mask,
        )

    zero = jnp.zeros((8, C), F32)
    column = jnp.zeros((40, 1), F32)
    gain_sum2, shift_sum2, misfit_sum, count = lax.fori_loop(0, 8, head_row, (zero, zero, column, column), unroll=8)
    lz = Exchange("z", Z, z, lambda p: LG.at[z, x, c], lambda s: LG.at[s, x, c], (lz_s, lz_r))
    lz.start()
    grad = gf[...]
    grad_late = pltpu.roll(grad, 1, 0)
    for h in range(2):
        G[h, 0] = grad[:, 256 * h : 256 * (h + 1)].astype(BF16)
        G[h, 1] = grad_late[:, 256 * h : 256 * (h + 1)].astype(BF16)
    g_send = core_copy(2, G.at[other], lambda s: g_peer)
    g_send.start()

    def column_grads(acts, grads):
        e, o = acts[:rows], acts[rows:]
        return dot(e, grads[0], TN), dot(o, grads[0], TN), dot(e, grads[1], TN)

    own = column_grads(act, G.at[c])
    lx = Exchange("x", X, x, lambda p: LG.at[:, x, c], lambda s: LG.at[:, s, c], (lx_s, lx_r))
    lc = core_copy(3, LG.at[:, :, c], lambda s: LG.at[:, :, s])
    act_send.wait_all_recv()
    g_send.wait_all_recv()
    peers = column_grads(act_peer, g_peer)
    total = jnp.concatenate([a + b for a, b in zip(own, peers)], axis=0)
    DA[...] = total[:, :128].reshape(Y, RY, 128)
    DB[...] = total[:, 128:].reshape(Y, Z, RZ, 128).transpose(1, 0, 2, 3).reshape(Z, Y * RZ, 128)
    def encode(full, coded):
        values = full[...]
        n, height, width = values.shape
        top = jnp.max(jnp.abs(values).reshape(n * height, width), axis=0, keepdims=True)
        power = power_of(top)
        ratio = jnp.exp(power * -LN2)
        coded[:, :height] = jnp.round(values * ratio[None]).astype(jnp.int32).astype(jnp.int16)
        code = jnp.broadcast_to(power, (16, width)).astype(jnp.int32).astype(jnp.int16)
        for k in range(n):
            coded[k, height:] = code

    def decoded(slot):
        height = slot.shape[0] - 16
        power = slot[height:, :].astype(jnp.int32).astype(F32)[0:1]
        return slot[:height, :].astype(jnp.int32).astype(F32) * jnp.exp(power * LN2)

    ya = Exchange("y", Y, y, lambda p: QA.at[p], lambda s: RA.at[s], (a_s, a_r))
    zb = Exchange("z", Z, z, lambda p: QB.at[p], lambda s: RB.at[s], (b_s, b_r))
    encode(DA, QA)
    ya.start()
    encode(DB, QB)
    zb.start()
    lz.wait_all_recv()
    lx.start()

    def whole_grad(k):
        return jnp.concatenate([G[0, k], G[1, k]], axis=1)

    now, late = whole_grad(0), whole_grad(1)
    dact[:rows] = dot(now, tap_weight(0), NT) + dot(late, tap_weight(2), NT)
    dact[rows:] = dot(now, tap_weight(1), NT)

    def backward_chunk(i, carry):
        gain_sum, shift_sum = carry
        at = pl.ds(pl.multiple_of(i * CHUNK, CHUNK), CHUNK)
        normed = xh[at, :]
        du = dact[at, :] * dg[at, :]
        dx = du * g1
        m1 = jnp.mean(dx, axis=1, keepdims=True)
        m2 = jnp.mean(dx * normed, axis=1, keepdims=True)
        dpre = rs[at, :1] * (dx - m1 - normed * m2)
        hi, mid = split2(dpre)
        gph[at, :] = hi
        gpm[at, :] = mid
        return gain_sum + fold8(du * normed), shift_sum + fold8(du)

    gain_sum1, shift_sum1 = lax.fori_loop(0, chunks, backward_chunk, (zero, zero), unroll=2)
    taps = dot(xcol[...], gph[...], TN) + dot(xcol[...], gpm[...], TN)
    ri = lax.broadcasted_iota(jnp.int32, (8, C), 0)
    li = lax.broadcasted_iota(jnp.int32, (8, C), 1)

    def line(vector, k):
        return jnp.where(ri == k, jnp.sum(vector, axis=0, keepdims=True), 0.0)

    loss_line = jnp.where(
        li == 0,
        jnp.sum(misfit_sum, axis=0, keepdims=True),
        jnp.where(li == 1, jnp.sum(count, axis=0, keepdims=True), 0.0),
    )
    groups = [
        taps[0:8] + taps[8:16],
        taps[32:40] + taps[40:48],
        line(gain_sum1, 0) + line(shift_sum1, 1) + line(gain_sum2, 2) + line(shift_sum2, 3)
        + jnp.where(ri == 4, loss_line, 0.0),
        zero,
    ]
    for i, group in enumerate(groups):
        for j in range(4):
            S[i // 2, 4 * (i % 2) + j] = group[:, 128 * j : 128 * (j + 1)]
    sc = core_copy(4, S.at[other], lambda s: S_peer)
    sc.start()
    lx.wait_all_recv()
    lc.start()
    sc.wait_all_recv()
    S1[...] = (S[c] + S_peer[...]).reshape(Y, per_y, 8, 128)
    sy = Exchange("y", Y, y, lambda p: S1.at[p], lambda s: SY.at[s], (sy_s, sy_r))
    sy.start()

    total = DA[y]
    for r in range(1, Y):
        ya.wait_recv(r)
        total = total + decoded(RA.at[ya.sender(r)])
    A1[...] = total.reshape(Z, RZ, 128)
    za = Exchange("z", Z, z, lambda p: A1.at[p], lambda s: RA2.at[s], (a2_s, a2_r))
    za.start()
    total = DB[z]
    for r in range(1, Z):
        zb.wait_recv(r)
        total = total + decoded(RB.at[zb.sender(r)])
    B1[...] = total.reshape(Y, RZ, 128)
    yb = Exchange("y", Y, y, lambda p: B1.at[p], lambda s: RB2.at[s], (b2_s, b2_r))
    yb.start()
    sy.wait_all_recv()
    SY[y] = S1[y]
    total = SY[0]
    for k in range(1, Y):
        total = total + SY[k]
    SZ[z] = total
    sz = Exchange("z", Z, z, lambda p: SZ.at[z], lambda s: SZ.at[s], (sz_s, sz_r))
    sz.start()

    first = A1[z]
    for r in range(1, Z):
        za.wait_recv(r)
        first = first + RA2[za.sender(r)]
    second = B1[y]
    for r in range(1, Y):
        yb.wait_recv(r)
        second = second + RB2[yb.sender(r)]
    XR[x] = jnp.concatenate([first, second], axis=1)
    xs = Exchange("x", X, x, lambda p: XR.at[x], lambda s: XR.at[s], (x_s, x_r))
    xs.start()
    sz.wait_all_recv()
    total = SZ[0]
    for k in range(1, Z):
        total = total + SZ[k]
    SX[x] = total
    sx = Exchange("x", X, x, lambda p: SX.at[x], lambda s: SX.at[s], (sx_s, sx_r))
    sx.start()

    xs.wait_all_recv()
    total = XR[0]
    for k in range(1, X):
        total = total + XR[k]
    power = power_of(jnp.max(jnp.abs(total), axis=0, keepdims=True))
    spare = FQ.shape[2] - RZ
    codes = jnp.concatenate(
        [jnp.round(total * jnp.exp(power * -LN2)), jnp.broadcast_to(power, (spare, 256))], axis=0
    )
    FQ[c, z] = codes.astype(jnp.int32).astype(jnp.int16)
    zg = Exchange("z", Z, z, lambda p: FQ.at[c, z], lambda s: FQ.at[c, s], (z_s, z_r))
    zg.start()
    sx.wait_all_recv()
    total = SX[0]
    for k in range(1, X):
        total = total + SX[k]
    SA[y] = total
    sa = Exchange("y", Y, y, lambda p: SA.at[y], lambda s: SA.at[s], (sa_s, sa_r))
    sa.start()

    lc.wait_all_recv()
    logs = LG[...].reshape(readers, 128)
    picked = sum(dot(pick[...], part, TN) for part in split3(logs))
    lv_ref[...] = picked[:8, : lv_ref.shape[1]]

    zg.wait_all_recv()
    fin = core_copy(5, FQ.at[c], lambda s: FQ.at[s])
    fin.start()

    sa.wait_all_recv()
    small_ref[c] = SA[...].reshape(TILES // 2, 8, 128)
    sf = core_copy(6, small_ref.at[c], lambda s: small_ref.at[s])
    sf.start()
    sf.wait_all_recv()
    fin.wait_all_recv()
    for h in range(2):
        for k in range(Z):
            piece = FQ[h, k].astype(jnp.int32).astype(F32)
            gw2_ref[k * RZ : (k + 1) * RZ, 256 * h : 256 * (h + 1)] = piece[:RZ] * jnp.exp(
                piece[RZ : RZ + 1] * LN2
            )

    waiting = [wy, wd, tc, tx, tz, act_send, g_send, lc, lx, lz, ya, zb, za, yb, xs, zg, sc, sy, sz, sx, sa, sf, fin]
    for e in waiting + wxs + wcs:
        e.wait_sends()


def write_kernel(lv_in, gw2_in, small, lv_ref, loss_ref, gw2_ref, gw1_ref, gg1_ref, gs1_ref, gg2_ref, gs2_ref):
    def wide(i):
        return jnp.concatenate([small[i // 2, 4 * (i % 2) + j] for j in range(4)], axis=1)

    lv_ref[...] = lv_in[...]
    gw2_ref[...] = gw2_in[...]
    gw1_ref[0:5] = wide(0)[0:5]
    gw1_ref[5:10] = wide(1)[0:5]
    norms = wide(2)
    gg1_ref[...] = norms[0:1]
    gs1_ref[...] = norms[1:2]
    gg2_ref[...] = norms[2:3]
    gs2_ref[...] = norms[3:4]
    loss_ref[...] = norms[4:5, 0:1] / norms[4:5, 1:2]


def per_device(sizes, waveform, lengths, owner_of, targets, first_weight, first_gain, first_shift,
               second_weight, second_gain, second_shift):
    Z, X, Y = sizes
    row_total, later = targets.shape
    RY = second_weight.shape[0]
    RZ = RY // Z
    rows = 320
    dma = pltpu.SemaphoreType.DMA
    vm = pltpu.VMEM
    per_y = TILES // 2 // Y
    scratch = [
        vm(waveform.shape, F32), vm(targets.shape, F32), pltpu.SMEM(owner_of.shape, jnp.int32),
        pltpu.SMEM(lengths.shape, jnp.int32), vm(first_weight.shape, F32), vm((1, C), F32), vm((1, C), F32),
        vm((1, C), F32), vm((1, C), F32), dma((10,)),
        vm((Y, RY, C), BF16), vm((Z, X, 2, 8, 128), F32), vm((Z, X, 2, 8, 128), F32), vm((8, 128), F32),
        vm((8, 512), F32), vm((128, C), F32), vm((2 * rows, 128), BF16),
        vm((2 * rows, C), F32), vm((2 * rows, C), F32), vm((2 * rows, 128), F32),
        vm((2 * rows, C), BF16), vm((2 * rows, C), BF16), vm((rows, C), F32),
        vm((8, 128), F32), vm((8, 128), F32), vm((rows, C), F32),
        vm((2, 2, rows, 256), BF16), vm((2, rows, 256), BF16),
        vm((Y, RY, 128), F32), vm((Z, Y * RZ, 128), F32),
        vm((Y, RY + 16, 128), jnp.int16), vm((Z, Y * RZ + 16, 128), jnp.int16),
        vm((Y, RY + 16, 128), jnp.int16), vm((Z, Y * RZ + 16, 128), jnp.int16),
        vm((Z, RZ, 128), F32), vm((Y, RZ, 128), F32), vm((Z, RZ, 128), F32), vm((Y, RZ, 128), F32),
        vm((X, RZ, 256), F32), vm((2 * rows, C), F32), vm((2 * rows, C), BF16), vm((2 * rows, C), BF16),
        vm((2, TILES // 2, 8, 128), F32), vm((TILES // 2, 8, 128), F32), vm((Y, per_y, 8, 128), F32),
        vm((Y, per_y, 8, 128), F32), vm((Z, per_y, 8, 128), F32), vm((X, per_y, 8, 128), F32),
        vm((Y, per_y, 8, 128), F32), vm((Z * X * 2 * 8, 128), BF16),
        vm((2, Z, RZ + (8 if RZ % 16 else 16), 256), jnp.int16),
        dma((Y,)), dma((Y,)), dma((Y,)), dma((Y,)), dma((Y, X)), dma((Y, X)), dma((Y, 2)), dma((Y, 2)),
        dma((X,)), dma((X,)), dma((Z,)), dma((Z,)), dma((X,)), dma((X,)), dma((Z,)), dma((Z,)),
        dma((Y,)), dma((Y,)), dma((Z,)), dma((Z,)), dma((Z,)), dma((Z,)), dma((Y,)), dma((Y,)),
        dma((X,)), dma((X,)), dma((Z,)), dma((Z,)),
        dma((Y,)), dma((Y,)), dma((Z,)), dma((Z,)), dma((X,)), dma((X,)), dma((Y,)), dma((Y,)),
        dma((8, 2)), dma((8, 2)),
    ]
    shapes = [
        (row_total, later), (1, 1), (RY, C), (10, C), (1, C), (1, C), (1, C), (1, C),
    ]
    whole = pl.BlockSpec(memory_space=pltpu.VMEM)
    sums = pl.pallas_call(
        functools.partial(kernel, sizes),
        out_shape=[jax.ShapeDtypeStruct(s, F32) for s in (shapes[0], shapes[2], (2, TILES // 2, 8, 128))],
        in_specs=[pl.BlockSpec(memory_space=pl.ANY)] * 10,
        out_specs=[whole] * 3,
        scratch_shapes=scratch,
        compiler_params=pltpu.CompilerParams(
            collective_id=0, has_side_effects=True, vmem_limit_bytes=56 * 2**20
        ),
    )(
        waveform, targets, owner_of, lengths, first_weight, first_gain[None], first_shift[None],
        second_weight, second_gain[None], second_shift[None],
    )
    out = pl.pallas_call(
        write_kernel,
        out_shape=[jax.ShapeDtypeStruct(s, F32) for s in shapes],
        in_specs=[whole] * 3,
        out_specs=[whole] * len(shapes),
    )(*sums)
    lv, loss, gw2, gw1, gg1, gs1, gg2, gs2 = out
    return lv, loss[0, 0], gw2, gw1, gg1[0], gs1[0], gg2[0], gs2[0]


def solution(mesh):
    dp, fsdp = mesh.shape["dp"], mesh.shape["fsdp"]
    x = 4 if dp >= 64 else 2
    z = dp // (2 * x)
    torus = Mesh(mesh.devices.reshape(z, x, 2, fsdp), ("dp_0", "dp_1", "dp_2", "fsdp"))
    return jax.shard_map(
        functools.partial(per_device, (z, x, fsdp)),
        mesh=torus,
        in_specs=(
            P(DP_FSDP, None), P(DP_FSDP), P(DP_FSDP), P(DP_FSDP, None), P(), P(), P(),
            P("fsdp", None), P(), P(),
        ),
        out_specs=(P(DP_FSDP, None), P(), P("fsdp", None), P(), P(), P(), P(), P()),
        check_vma=False,
    )
```

```python
import functools

import jax
import jax.numpy as jnp
from jax import lax
from jax.experimental import pallas as pl
from jax.experimental.pallas import tpu as pltpu
from jax.sharding import Mesh
from jax.sharding import PartitionSpec as P

DP = ("dp_0", "dp_1", "dp_2")
DP_FSDP = ("dp_0", "dp_1", "dp_2", "fsdp")
AXES = {"z": "dp_0", "x": "dp_1", "c": "dp_2", "y": "fsdp"}
EPS = 1e-05
C = 512
F32 = jnp.float32
BF16 = jnp.bfloat16
MESH = pl.DeviceIdType.MESH
TN = (((0,), (0,)), ((), ()))
NT = (((1,), (1,)), ((), ()))
TILES = 16
CHUNK = 32
LN2 = 0.6931471805599453
LOG2E = 1.4426950408889634


class Exchange:
    def __init__(self, axis, size, me, src, dst, sems):
        self.axis, self.size, self.me = axis, size, me
        self.src, self.dst = src, dst
        self.send_sems, self.recv_sems = sems

    def _copy(self, r, slot, peer):
        return pltpu.make_async_remote_copy(
            src_ref=self.src(peer),
            dst_ref=self.dst(slot),
            send_sem=self.send_sems.at[r],
            recv_sem=self.recv_sems.at[r],
            device_id={AXES[self.axis]: peer},
            device_id_type=MESH,
        )

    def start(self):
        for r in sorted(range(1, self.size), key=lambda r: -min(r, self.size - r)):
            self._copy(r, self.me, lax.rem(self.me + r, self.size)).start()

    def sender(self, r):
        return lax.rem(self.me + self.size - r, self.size)

    def wait_recv(self, r):
        s = self.sender(r)
        self._copy(r, s, s).wait_recv()

    def wait_all_recv(self):
        for r in range(1, self.size):
            self.wait_recv(r)

    def wait_sends(self):
        for r in range(1, self.size):
            self._copy(r, self.me, lax.rem(self.me + r, self.size)).wait_send()


def dot(a, b, dims=(((1,), (0,)), ((), ()))):
    return lax.dot_general(a, b, dims, preferred_element_type=F32)


def split2(v):
    hi = v.astype(BF16)
    return hi, (v - hi.astype(F32)).astype(BF16)


def split3(v):
    hi, mid = split2(v)
    return hi, mid, (v - hi.astype(F32) - mid.astype(F32)).astype(BF16)


def gelu_parts(u):
    a = jnp.abs(u)
    t = 1.0 / (1.0 + 0.23164190 * a)
    e = jnp.exp(u * u * -0.5)
    poly = 0.5 * 1.061405429
    poly = poly * t - 0.5 * 1.453152027
    poly = poly * t + 0.5 * 1.421413741
    poly = poly * t - 0.5 * 0.284496736
    poly = poly * t + 0.5 * 0.254829592
    tail = poly * t * e
    cdf = jnp.where(u >= 0.0, 1.0 - tail, tail)
    return u * cdf, cdf + u * (e * 0.3989422804014327)


def power_of(top):
    return jnp.ceil(jnp.log(jnp.maximum(top, 1e-30)) * LOG2E + 0.01) - 15.0


def fold8(v):
    return v.reshape(v.shape[0] // 8, 8, v.shape[1]).sum(axis=0)


def kernel(sizes, *refs):
    Z, X, Y = sizes
    (wave_in, tgt_in, own_in, len_in, fw_in, g1_in, s1_in, w_in, g2_in, s2_in,
     lv_ref, gw2_ref, small_ref,
     wave_ref, tgt_ref, own_ref, len_ref, fw_ref, g1_ref, s1_ref, g2_ref, s2_ref, in_s,
     W, TG, LG, blk, wpad, wconv, xcol, xh, dg, rs, act, act_peer, v, tsel, vmask, gf, G, g_peer,
     DA, DB, QA, QB, RA, RB, A1, B1, RA2, RB2, XR, dact, gph, gpm, S, S_peer, SY, S1, SZ, SX, SA, pick, FQ,
     w_sy, w_ry, w_sd, w_rd, w_sx, w_rx, w_sc, w_rc, tx_s, tx_r, tz_s, tz_r, lx_s, lx_r, lz_s, lz_r,
     a_s, a_r, b_s, b_r, a2_s, a2_r, b2_s, b2_r, x_s, x_r, z_s, z_r,
     sy_s, sy_r, sz_s, sz_r, sx_s, sx_r, sa_s, sa_r, c_s, c_r) = refs
    z, x, c, y = (lax.axis_index(AXES[k]) for k in "zxcy")
    other = 1 - c
    RY = W.shape[1]
    routed = RY // 2
    halves = X // 2
    RX = routed // halves
    RZ = RY // Z
    rows = 8 * 40
    per_y = TILES // 2 // Y
    dp = Z * X * 2
    readers = dp * 8
    me_dp = (z * X + x) * 2 + c

    barrier = pltpu.get_barrier_semaphore()
    for axis, size, me in (("c", 2, c), ("x", X, x), ("y", Y, y), ("z", Z, z)):
        for r in range(1, size):
            pl.semaphore_signal(
                barrier, inc=1, device_id={AXES[axis]: lax.rem(me + r, size)}, device_id_type=MESH
            )

    def core_copy(k, src, dst):
        return Exchange("c", 2, c, lambda p: src, dst, (c_s.at[k], c_r.at[k]))

    half = pl.ds(pl.multiple_of(c * 256, 256), 256)

    loads = [
        pltpu.make_async_copy(source, target, in_s.at[k])
        for k, (source, target) in enumerate(
            (
                (w_in, W.at[y]), (own_in, own_ref), (len_in, len_ref), (tgt_in, tgt_ref), (wave_in, wave_ref),
                (fw_in, fw_ref), (g1_in, g1_ref), (s1_in, s1_ref), (g2_in, g2_ref), (s2_in, s2_ref),
            )
        )
    ]
    for load in loads:
        load.start()
    for load in loads[:4]:
        load.wait()
    r8 = lax.broadcasted_iota(jnp.int32, (8, 128), 0)
    l8 = lax.broadcasted_iota(jnp.int32, (8, 128), 1)
    numbers = jnp.zeros((8, 128), jnp.int32)
    for k in range(8):
        valid = ((len_ref[k] - 10) // 5 - 2) // 2 + 1
        numbers = jnp.where(r8 == k, jnp.where(l8 == 39, own_ref[k], valid), numbers)
    blk[...] = numbers.astype(F32)
    blk[:, : tgt_ref.shape[1]] = tgt_ref[...]
    TG[z, x, c] = blk[...]

    def part_rows(k):
        return pl.ds(pl.multiple_of(k % halves * RX, 16), RX)

    def part_lanes(k):
        return pl.ds(pl.multiple_of(c * 256 + k // halves * 128, 128), 128)

    pl.semaphore_wait(barrier, 1 + (X - 1) + (Y - 1) + (Z - 1))

    wy = Exchange(
        "y", Y, y, lambda p: W.at[y, part_rows(x), part_lanes(x)],
        lambda s: W.at[s, part_rows(x), part_lanes(x)], (w_sy, w_ry),
    )
    wy.start()
    rest = pl.ds(routed, RY - routed)
    wd = Exchange("y", Y, y, lambda p: W.at[y, rest, half], lambda s: W.at[s, rest, half], (w_sd, w_rd))

    def wx(k, slot):
        return Exchange(
            "x", X, x, lambda p: W.at[slot, part_rows(x), part_lanes(x)],
            lambda s: W.at[slot, part_rows(s), part_lanes(s)], (w_sx.at[k], w_rx.at[k]),
        )

    def half_of(k):
        return pl.ds(pl.multiple_of(k * 256, 256), 256)

    def wc(k, slot):
        return Exchange(
            "c", 2, c, lambda p: W.at[slot, :, half], lambda s: W.at[slot, :, half_of(s)],
            (w_sc.at[k], w_rc.at[k]),
        )

    wxs = [wx(r, wy.sender(r)) for r in range(1, Y)]
    wcs = [wc(r, wy.sender(r)) for r in range(1, Y)]
    tz = Exchange("z", Z, z, lambda p: TG.at[z, x, c], lambda s: TG.at[s, x, c], (tz_s, tz_r))
    tz.start()
    tx = Exchange("x", X, x, lambda p: TG.at[:, x, c], lambda s: TG.at[:, s, c], (tx_s, tx_r))
    tc = core_copy(0, TG.at[:, :, c], lambda s: TG.at[:, :, s])

    for load in loads[4:]:
        load.wait()
    wpad[...] = jnp.zeros_like(wpad)
    wpad[:, : wave_ref.shape[1]] = wave_ref[...]
    samples = lax.broadcasted_iota(jnp.int32, (512, 128), 0).astype(F32)
    lanes = lax.broadcasted_iota(jnp.int32, (512, 128), 1).astype(F32)
    tap = samples - 5.0 * jnp.floor((samples + 0.5) * 0.2)
    place_hi = jnp.where((lanes == tap) | (lanes == tap + 16.0), 1.0, 0.0).astype(BF16)
    place_mid = jnp.where(lanes == tap + 8.0, 1.0, 0.0).astype(BF16)
    frame = lax.broadcasted_iota(jnp.int32, (40, 512), 0)
    offset = lax.broadcasted_iota(jnp.int32, (40, 512), 1) - 10 * frame
    in_even = (offset >= 0) & (offset < 5)
    in_odd = (offset >= 5) & (offset < 10)
    even, odd = [], []
    for k in range(8):
        row = jnp.broadcast_to(wpad[k : k + 1, :], (40, 512))
        even.append(jnp.where(in_even, row, 0.0))
        odd.append(jnp.where(in_odd, row, 0.0))
    blocks = []
    for parts in (even, odd):
        hi, mid = split2(jnp.concatenate(parts, axis=0))
        blocks.append(dot(hi, place_hi) + dot(mid, place_mid))
    even_block, odd_block = blocks
    xcol[:rows] = (even_block + pltpu.roll(odd_block, 32, 1)).astype(BF16)
    xcol[rows:] = (odd_block + pltpu.roll(pltpu.roll(even_block, rows - 1, 0), 32, 1)).astype(BF16)
    wconv[...] = jnp.zeros_like(wconv)
    fw = fw_ref[...]
    fw_hi = fw.astype(BF16).astype(F32)
    fw_mid = (fw - fw_hi).astype(BF16).astype(F32)
    for base, taps in ((0, slice(0, 5)), (32, slice(5, 10))):
        wconv[base : base + 5] = fw_hi[taps]
        wconv[base + 8 : base + 13] = fw_hi[taps]
        wconv[base + 16 : base + 21] = fw_mid[taps]
    xh[...] = dot(xcol[...], wconv[...].astype(BF16))

    wd.start()
    g1, s1 = g1_ref[...], s1_ref[...]

    def forward_chunk(i, carry):
        at = pl.ds(pl.multiple_of(i * CHUNK, CHUNK), CHUNK)
        pre = xh[at, :]
        centered = pre - jnp.mean(pre, axis=1, keepdims=True)
        inv = lax.rsqrt(jnp.mean(centered * centered, axis=1, keepdims=True) + EPS)
        normed = centered * inv
        value, slope = gelu_parts(normed * g1 + s1)
        xh[at, :] = normed
        dg[at, :] = slope
        rs[at, :] = jnp.broadcast_to(inv, (CHUNK, 128))
        act[at, :] = value.astype(BF16)
        return carry

    chunks = 2 * rows // CHUNK
    near_first = sorted(range(1, Y), key=lambda r: min(r, Y - r))
    steps = 4
    for k in range(steps):
        for r in near_first[k * 2 : (k + 1) * 2 if k < 2 else Y] if k < 3 else ():
            wy.wait_recv(r)
            wxs[r - 1].start()
        if k == 1:
            tz.wait_all_recv()
            tx.start()
        if k == 3:
            tx.wait_all_recv()
            tc.start()
        lax.fori_loop(chunks * k // steps, chunks * (k + 1) // steps, forward_chunk, 0, unroll=True)
    act_send = core_copy(1, act, lambda s: act_peer)
    act_send.start()
    for r in near_first:
        wxs[r - 1].wait_all_recv()
        wd.wait_recv(r)
        wcs[r - 1].start()

    tc.wait_all_recv()
    table = TG[...].reshape(readers, 128)
    owner_col = table[:, 39:40]
    mine = blk[...]
    owner_row = jnp.sum(jnp.where(r8 == l8, mine[:, 39:40], 0.0), axis=0, keepdims=True)
    rr = lax.broadcasted_iota(jnp.int32, (readers, 128), 0)
    ll = lax.broadcasted_iota(jnp.int32, (readers, 128), 1)
    before = jnp.sum(
        jnp.where((owner_col == owner_row) & (rr < me_dp * 8), 1.0, 0.0), axis=0, keepdims=True
    )
    wanted = owner_row * 8.0 + before
    one_hot = jnp.where((rr.astype(F32) == wanted) & (ll < 8), 1.0, 0.0).astype(BF16)
    found = sum(dot(one_hot, part, TN) for part in split3(table))
    tsel[...] = found[:8]
    vmask[...] = jnp.where(l8.astype(F32) < mine[:, 40:41], 1.0, 0.0)
    flags = jnp.where(owner_col == me_dp.astype(F32), 1.0, 0.0)
    flags = jnp.broadcast_to(flags, (readers, 128))
    lower = lax.broadcasted_iota(jnp.int32, (readers, readers), 0) > lax.broadcasted_iota(
        jnp.int32, (readers, readers), 1
    )
    place = dot(jnp.where(lower, 1.0, 0.0).astype(BF16), flags.astype(BF16))
    pick[...] = jnp.where((flags > 0.5) & (place == ll.astype(F32)), 1.0, 0.0).astype(BF16)

    for e in wcs:
        e.wait_all_recv()

    def tap_weight(q):
        return W[...].reshape(3 * C, C)[q * C : (q + 1) * C]

    act_even, act_odd = act[:rows], act[rows:]
    later = dot(act_even, tap_weight(2))
    v[...] = dot(act_even, tap_weight(0)) + dot(act_odd, tap_weight(1)) + pltpu.roll(later, rows - 1, 0)

    g2, s2 = g2_ref[...], s2_ref[...]
    eye = lax.broadcasted_iota(jnp.int32, (40, 128), 0) == lax.broadcasted_iota(jnp.int32, (40, 128), 1)

    def head_row(k, carry):
        gain_sum, shift_sum, misfit_sum, count = carry
        at = pl.ds(pl.multiple_of(k * 40, 8), 40)
        target = jnp.sum(jnp.where(eye, tsel[pl.ds(k, 1), :], 0.0), axis=1, keepdims=True)
        mask = jnp.sum(jnp.where(eye, vmask[pl.ds(k, 1), :], 0.0), axis=1, keepdims=True)
        pre = v[at, :]
        centered = pre - jnp.mean(pre, axis=1, keepdims=True)
        inv = lax.rsqrt(jnp.mean(centered * centered, axis=1, keepdims=True) + EPS)
        normed = centered * inv
        value, slope = gelu_parts(normed * g2 + s2)
        centered = value - jnp.mean(value, axis=1, keepdims=True)
        spread = jnp.mean(centered * centered, axis=1, keepdims=True) + EPS
        raw = jnp.log(spread)
        misfit = raw - target
        LG[z, x, c, pl.ds(k, 1), :] = jnp.sum(jnp.where(eye, raw * mask, 0.0), axis=0, keepdims=True)
        du = centered * (mask * misfit * (4.0 / C) / spread) * slope
        dx = du * g2
        m1 = jnp.mean(dx, axis=1, keepdims=True)
        m2 = jnp.mean(dx * normed, axis=1, keepdims=True)
        gf[at, :] = inv * (dx - m1 - normed * m2)
        return (
            gain_sum + fold8(du * normed),
            shift_sum + fold8(du),
            misfit_sum + mask * misfit * misfit,
            count + mask,
        )

    zero = jnp.zeros((8, C), F32)
    column = jnp.zeros((40, 1), F32)
    gain_sum2, shift_sum2, misfit_sum, count = lax.fori_loop(0, 8, head_row, (zero, zero, column, column), unroll=8)
    lz = Exchange("z", Z, z, lambda p: LG.at[z, x, c], lambda s: LG.at[s, x, c], (lz_s, lz_r))
    lz.start()
    grad = gf[...]
    grad_late = pltpu.roll(grad, 1, 0)
    for h in range(2):
        G[h, 0] = grad[:, 256 * h : 256 * (h + 1)].astype(BF16)
        G[h, 1] = grad_late[:, 256 * h : 256 * (h + 1)].astype(BF16)
    g_send = core_copy(2, G.at[other], lambda s: g_peer)
    g_send.start()

    def column_grads(acts, grads):
        e, o = acts[:rows], acts[rows:]
        return dot(e, grads[0], TN), dot(o, grads[0], TN), dot(e, grads[1], TN)

    own = column_grads(act, G.at[c])
    lx = Exchange("x", X, x, lambda p: LG.at[:, x, c], lambda s: LG.at[:, s, c], (lx_s, lx_r))
    lc = core_copy(3, LG.at[:, :, c], lambda s: LG.at[:, :, s])
    act_send.wait_all_recv()
    g_send.wait_all_recv()
    peers = column_grads(act_peer, g_peer)
    total = jnp.concatenate([a + b for a, b in zip(own, peers)], axis=0)
    DA[...] = total[:, :128].reshape(Y, RY, 128)
    DB[...] = total[:, 128:].reshape(Y, Z, RZ, 128).transpose(1, 0, 2, 3).reshape(Z, Y * RZ, 128)
    def encode(full, coded):
        values = full[...]
        n, height, width = values.shape
        top = jnp.max(jnp.abs(values).reshape(n * height, width), axis=0, keepdims=True)
        power = power_of(top)
        ratio = jnp.exp(power * -LN2)
        coded[:, :height] = jnp.round(values * ratio[None]).astype(jnp.int32).astype(jnp.int16)
        code = jnp.broadcast_to(power, (16, width)).astype(jnp.int32).astype(jnp.int16)
        for k in range(n):
            coded[k, height:] = code

    def decoded(slot):
        height = slot.shape[0] - 16
        power = slot[height:, :].astype(jnp.int32).astype(F32)[0:1]
        return slot[:height, :].astype(jnp.int32).astype(F32) * jnp.exp(power * LN2)

    ya = Exchange("y", Y, y, lambda p: QA.at[p], lambda s: RA.at[s], (a_s, a_r))
    zb = Exchange("z", Z, z, lambda p: QB.at[p], lambda s: RB.at[s], (b_s, b_r))
    encode(DA, QA)
    ya.start()
    encode(DB, QB)
    zb.start()
    lz.wait_all_recv()
    lx.start()

    def whole_grad(k):
        return jnp.concatenate([G[0, k], G[1, k]], axis=1)

    now, late = whole_grad(0), whole_grad(1)
    dact[:rows] = dot(now, tap_weight(0), NT) + dot(late, tap_weight(2), NT)
    dact[rows:] = dot(now, tap_weight(1), NT)

    def backward_chunk(i, carry):
        gain_sum, shift_sum = carry
        at = pl.ds(pl.multiple_of(i * CHUNK, CHUNK), CHUNK)
        normed = xh[at, :]
        du = dact[at, :] * dg[at, :]
        dx = du * g1
        m1 = jnp.mean(dx, axis=1, keepdims=True)
        m2 = jnp.mean(dx * normed, axis=1, keepdims=True)
        dpre = rs[at, :1] * (dx - m1 - normed * m2)
        hi, mid = split2(dpre)
        gph[at, :] = hi
        gpm[at, :] = mid
        return gain_sum + fold8(du * normed), shift_sum + fold8(du)

    gain_sum1, shift_sum1 = lax.fori_loop(0, chunks, backward_chunk, (zero, zero), unroll=2)
    taps = dot(xcol[...], gph[...], TN) + dot(xcol[...], gpm[...], TN)
    ri = lax.broadcasted_iota(jnp.int32, (8, C), 0)
    li = lax.broadcasted_iota(jnp.int32, (8, C), 1)

    def line(vector, k):
        return jnp.where(ri == k, jnp.sum(vector, axis=0, keepdims=True), 0.0)

    loss_line = jnp.where(
        li == 0,
        jnp.sum(misfit_sum, axis=0, keepdims=True),
        jnp.where(li == 1, jnp.sum(count, axis=0, keepdims=True), 0.0),
    )
    groups = [
        taps[0:8] + taps[8:16],
        taps[32:40] + taps[40:48],
        line(gain_sum1, 0) + line(shift_sum1, 1) + line(gain_sum2, 2) + line(shift_sum2, 3)
        + jnp.where(ri == 4, loss_line, 0.0),
        zero,
    ]
    for i, group in enumerate(groups):
        for j in range(4):
            S[i // 2, 4 * (i % 2) + j] = group[:, 128 * j : 128 * (j + 1)]
    sc = core_copy(4, S.at[other], lambda s: S_peer)
    sc.start()
    lx.wait_all_recv()
    lc.start()
    sc.wait_all_recv()
    S1[...] = (S[c] + S_peer[...]).reshape(Y, per_y, 8, 128)
    sy = Exchange("y", Y, y, lambda p: S1.at[p], lambda s: SY.at[s], (sy_s, sy_r))
    sy.start()

    total = DA[y]
    for r in range(1, Y):
        ya.wait_recv(r)
        total = total + decoded(RA.at[ya.sender(r)])
    A1[...] = total.reshape(Z, RZ, 128)
    za = Exchange("z", Z, z, lambda p: A1.at[p], lambda s: RA2.at[s], (a2_s, a2_r))
    za.start()
    total = DB[z]
    for r in range(1, Z):
        zb.wait_recv(r)
        total = total + decoded(RB.at[zb.sender(r)])
    B1[...] = total.reshape(Y, RZ, 128)
    yb = Exchange("y", Y, y, lambda p: B1.at[p], lambda s: RB2.at[s], (b2_s, b2_r))
    yb.start()
    sy.wait_all_recv()
    SY[y] = S1[y]
    total = SY[0]
    for k in range(1, Y):
        total = total + SY[k]
    SZ[z] = total
    sz = Exchange("z", Z, z, lambda p: SZ.at[z], lambda s: SZ.at[s], (sz_s, sz_r))
    sz.start()

    first = A1[z]
    for r in range(1, Z):
        za.wait_recv(r)
        first = first + RA2[za.sender(r)]
    second = B1[y]
    for r in range(1, Y):
        yb.wait_recv(r)
        second = second + RB2[yb.sender(r)]
    XR[x] = jnp.concatenate([first, second], axis=1)
    xs = Exchange("x", X, x, lambda p: XR.at[x], lambda s: XR.at[s], (x_s, x_r))
    xs.start()
    sz.wait_all_recv()
    total = SZ[0]
    for k in range(1, Z):
        total = total + SZ[k]
    SX[x] = total
    sx = Exchange("x", X, x, lambda p: SX.at[x], lambda s: SX.at[s], (sx_s, sx_r))
    sx.start()

    xs.wait_all_recv()
    total = XR[0]
    for k in range(1, X):
        total = total + XR[k]
    power = power_of(jnp.max(jnp.abs(total), axis=0, keepdims=True))
    spare = FQ.shape[2] - RZ
    codes = jnp.concatenate(
        [jnp.round(total * jnp.exp(power * -LN2)), jnp.broadcast_to(power, (spare, 256))], axis=0
    )
    FQ[c, z] = codes.astype(jnp.int32).astype(jnp.int16)
    zg = Exchange("z", Z, z, lambda p: FQ.at[c, z], lambda s: FQ.at[c, s], (z_s, z_r))
    zg.start()
    sx.wait_all_recv()
    total = SX[0]
    for k in range(1, X):
        total = total + SX[k]
    SA[y] = total
    sa = Exchange("y", Y, y, lambda p: SA.at[y], lambda s: SA.at[s], (sa_s, sa_r))
    sa.start()

    lc.wait_all_recv()
    logs = LG[...].reshape(readers, 128)
    picked = sum(dot(pick[...], part, TN) for part in split3(logs))
    lv_ref[...] = picked[:8, : lv_ref.shape[1]]

    zg.wait_all_recv()
    fin = core_copy(5, FQ.at[c], lambda s: FQ.at[s])
    fin.start()

    sa.wait_all_recv()
    small_ref[c] = SA[...].reshape(TILES // 2, 8, 128)
    sf = core_copy(6, small_ref.at[c], lambda s: small_ref.at[s])
    sf.start()
    sf.wait_all_recv()
    fin.wait_all_recv()
    for h in range(2):
        for k in range(Z):
            piece = FQ[h, k].astype(jnp.int32).astype(F32)
            gw2_ref[k * RZ : (k + 1) * RZ, 256 * h : 256 * (h + 1)] = piece[:RZ] * jnp.exp(
                piece[RZ : RZ + 1] * LN2
            )

    waiting = [wy, wd, tc, tx, tz, act_send, g_send, lc, lx, lz, ya, zb, za, yb, xs, zg, sc, sy, sz, sx, sa, sf, fin]
    for e in waiting + wxs + wcs:
        e.wait_sends()


def write_kernel(lv_in, gw2_in, small, lv_ref, loss_ref, gw2_ref, gw1_ref, gg1_ref, gs1_ref, gg2_ref, gs2_ref):
    def wide(i):
        return jnp.concatenate([small[i // 2, 4 * (i % 2) + j] for j in range(4)], axis=1)

    lv_ref[...] = lv_in[...]
    gw2_ref[...] = gw2_in[...]
    gw1_ref[0:5] = wide(0)[0:5]
    gw1_ref[5:10] = wide(1)[0:5]
    norms = wide(2)
    gg1_ref[...] = norms[0:1]
    gs1_ref[...] = norms[1:2]
    gg2_ref[...] = norms[2:3]
    gs2_ref[...] = norms[3:4]
    loss_ref[...] = norms[4:5, 0:1] / norms[4:5, 1:2]


def per_device(sizes, waveform, lengths, owner_of, targets, first_weight, first_gain, first_shift,
               second_weight, second_gain, second_shift):
    Z, X, Y = sizes
    row_total, later = targets.shape
    RY = second_weight.shape[0]
    RZ = RY // Z
    rows = 320
    dma = pltpu.SemaphoreType.DMA
    vm = pltpu.VMEM
    per_y = TILES // 2 // Y
    scratch = [
        vm(waveform.shape, F32), vm(targets.shape, F32), pltpu.SMEM(owner_of.shape, jnp.int32),
        pltpu.SMEM(lengths.shape, jnp.int32), vm(first_weight.shape, F32), vm((1, C), F32), vm((1, C), F32),
        vm((1, C), F32), vm((1, C), F32), dma((10,)),
        vm((Y, RY, C), BF16), vm((Z, X, 2, 8, 128), F32), vm((Z, X, 2, 8, 128), F32), vm((8, 128), F32),
        vm((8, 512), F32), vm((128, C), F32), vm((2 * rows, 128), BF16),
        vm((2 * rows, C), F32), vm((2 * rows, C), F32), vm((2 * rows, 128), F32),
        vm((2 * rows, C), BF16), vm((2 * rows, C), BF16), vm((rows, C), F32),
        vm((8, 128), F32), vm((8, 128), F32), vm((rows, C), F32),
        vm((2, 2, rows, 256), BF16), vm((2, rows, 256), BF16),
        vm((Y, RY, 128), F32), vm((Z, Y * RZ, 128), F32),
        vm((Y, RY + 16, 128), jnp.int16), vm((Z, Y * RZ + 16, 128), jnp.int16),
        vm((Y, RY + 16, 128), jnp.int16), vm((Z, Y * RZ + 16, 128), jnp.int16),
        vm((Z, RZ, 128), F32), vm((Y, RZ, 128), F32), vm((Z, RZ, 128), F32), vm((Y, RZ, 128), F32),
        vm((X, RZ, 256), F32), vm((2 * rows, C), F32), vm((2 * rows, C), BF16), vm((2 * rows, C), BF16),
        vm((2, TILES // 2, 8, 128), F32), vm((TILES // 2, 8, 128), F32), vm((Y, per_y, 8, 128), F32),
        vm((Y, per_y, 8, 128), F32), vm((Z, per_y, 8, 128), F32), vm((X, per_y, 8, 128), F32),
        vm((Y, per_y, 8, 128), F32), vm((Z * X * 2 * 8, 128), BF16),
        vm((2, Z, RZ + (8 if RZ % 16 else 16), 256), jnp.int16),
        dma((Y,)), dma((Y,)), dma((Y,)), dma((Y,)), dma((Y, X)), dma((Y, X)), dma((Y, 2)), dma((Y, 2)),
        dma((X,)), dma((X,)), dma((Z,)), dma((Z,)), dma((X,)), dma((X,)), dma((Z,)), dma((Z,)),
        dma((Y,)), dma((Y,)), dma((Z,)), dma((Z,)), dma((Z,)), dma((Z,)), dma((Y,)), dma((Y,)),
        dma((X,)), dma((X,)), dma((Z,)), dma((Z,)),
        dma((Y,)), dma((Y,)), dma((Z,)), dma((Z,)), dma((X,)), dma((X,)), dma((Y,)), dma((Y,)),
        dma((8, 2)), dma((8, 2)),
    ]
    shapes = [
        (row_total, later), (1, 1), (RY, C), (10, C), (1, C), (1, C), (1, C), (1, C),
    ]
    whole = pl.BlockSpec(memory_space=pltpu.VMEM)
    sums = pl.pallas_call(
        functools.partial(kernel, sizes),
        out_shape=[vm(s, F32) for s in (shapes[0], shapes[2], (2, TILES // 2, 8, 128))],
        in_specs=[pl.BlockSpec(memory_space=pl.ANY)] * 10,
        out_specs=[whole] * 3,
        scratch_shapes=scratch,
        compiler_params=pltpu.CompilerParams(
            collective_id=0, has_side_effects=True, vmem_limit_bytes=56 * 2**20
        ),
    )(
        waveform, targets, owner_of, lengths, first_weight, first_gain[None], first_shift[None],
        second_weight, second_gain[None], second_shift[None],
    )
    out = pl.pallas_call(
        write_kernel,
        out_shape=[jax.ShapeDtypeStruct(s, F32) for s in shapes],
        in_specs=[whole] * 3,
        out_specs=[whole] * len(shapes),
    )(*[pltpu.with_memory_space_constraint(a, pltpu.VMEM) for a in sums])
    lv, loss, gw2, gw1, gg1, gs1, gg2, gs2 = out
    return lv, loss[0, 0], gw2, gw1, gg1[0], gs1[0], gg2[0], gs2[0]


def solution(mesh):
    dp, fsdp = mesh.shape["dp"], mesh.shape["fsdp"]
    x = 4 if dp >= 64 else 2
    z = dp // (2 * x)
    torus = Mesh(mesh.devices.reshape(z, x, 2, fsdp), ("dp_0", "dp_1", "dp_2", "fsdp"))
    return jax.shard_map(
        functools.partial(per_device, (z, x, fsdp)),
        mesh=torus,
        in_specs=(
            P(DP_FSDP, None), P(DP_FSDP), P(DP_FSDP), P(DP_FSDP, None), P(), P(), P(),
            P("fsdp", None), P(), P(),
        ),
        out_specs=(P(DP_FSDP, None), P(), P("fsdp", None), P(), P(), P(), P(), P()),
        check_vma=False,
    )
```
